256 devices in a mesh: dp: 32 (over x, y, core), tensor: 8 (over z).
Axes of the slice: x: 4, y: 4, z: 8, core: 2. Of those that a mesh axis runs over, the one named last changes fastest.
Arguments:
- queries: bfloat16 [4096, 8192], P('dp', 'tensor'), may hold values from -6 to 6
- resp_kv: bfloat16 [4096, 8, 256], P('dp', 'tensor'), may hold values from -6 to 6
- prompt_kv: bfloat16 [8192, 8, 256], P(('dp', 'tensor')), may hold values from -6 to 6
- resp_prompt: int32 [32, 4], P('dp'), may hold values from 0 to 7
- row_segment: int32 [32, 128], P('dp'), may hold values from 0 to 3, never falling along the last dimension, each value on 1 to 64 neighbouring positions
- cotangent: bfloat16 [4096, 8192], P('dp', 'tensor'), may hold values from -6 to 6
Outputs:
- attended: bfloat16 [4096, 8192], P('dp', 'tensor')
- query_grad: bfloat16 [4096, 8192], P('dp', 'tensor')
- resp_kv_grad: bfloat16 [4096, 8, 256], P('dp', 'tensor')
- prompt_kv_grad: float32 [8192, 8, 256], P(('dp', 'tensor'))
The draws below stay inside these ranges and needn't reach their ends.
Inputs may be any that keep to these rules, and one draw needn't show every extreme that they name: `row_segment`: in each block of 128 tokens, response numbers never fall and each of the 4 responses holds 1 to 64 tokens.
All inputs are finite; a program needn't handle non-finite values.
Results may differ from the reference program's by a relative error of at most 0.017.
Values may be sent and summed in bfloat16 or wider, within the bound.
A program may use at most 128 MiB of HBM per device.

```python
import math
import jax
import jax.numpy as jnp
import numpy as np
from jax import lax

HD = 128
HEADS = 64
KVH = 8
PLEN = 1024
ROWS_DEV = 128
RESP_DEV = 4
PROMPTS = 8
TOKENS = 4096
PROWS = 8192
N_DP = 32


def draw_queries(key, part):
    key = jax.random.fold_in(key, 11)
    values = jnp.clip(jax.random.normal(key, (TOKENS, HEADS * HD), jnp.float32), -6.0, 6.0)
    return values.astype(jnp.bfloat16)


def draw_prompt_kv(key, part):
    key = jax.random.fold_in(key, 12)
    values = jnp.clip(jax.random.normal(key, (PROWS, KVH, 2 * HD), jnp.float32), -6.0, 6.0)
    return values.astype(jnp.bfloat16)


def plant(array, key, low, top_value):
    longest = array.shape.index(max(array.shape))
    spots = []
    for shift in (0, 1):
        where = [jax.random.randint(jax.random.fold_in(key, axis), (), 0, length) for axis, length in enumerate(array.shape)]
        where[longest] = (where[longest] + shift) % array.shape[longest]
        spots.append(tuple(where))
    return array.at[spots[0]].set(low).at[spots[1]].set(top_value)


def level_of(key, dims, split, least, high):
    gain, own = 1.0, jax.random.fold_in(key, 6)
    for dim, parts in split:
        draws = jnp.exp(jax.random.uniform(jax.random.fold_in(own, dim), (parts,), jnp.float32, least / len(split), high / len(split)))
        gain = gain * jnp.repeat(draws, dims[dim] // parts).reshape([-1 if axis == dim else 1 for axis in range(len(dims))])
    return gain


def length_profile(number_of, total, most, skew):
    weights = [(1 << 20) // math.isqrt(standing ** skew) + 1 for standing in range(2, number_of + 1)]
    rest, given = total - most - (number_of - 1), [1] * (number_of - 1)
    while rest > 0:
        movable = [i for i in range(number_of - 1) if given[i] < most]
        pool, remaining = sum([weights[i] for i in movable]), rest
        for i in movable:
            more = min(most - given[i], max(1, remaining * weights[i] // pool), rest)
            given[i] = given[i] + more
            rest = rest - more
    return np.array([most] + given)


def ragged_sizes(own_key, amount, total, reach, skew):
    if amount == 2:
        one = jax.random.randint(own_key, (), max(1, total - reach), min(reach, total - 1) + 1)
        return jnp.stack([one, total - one])
    tallies = jnp.asarray(length_profile(amount, total, reach, skew), jnp.int32)
    pairs = (amount - 1) // 2
    giver, receiver = tallies[1:1 + 2 * pairs:2], tallies[2:2 + 2 * pairs:2]
    slack = jnp.minimum(giver - 1, reach - receiver)
    passed = jax.random.randint(jax.random.fold_in(own_key, 1), (pairs,), 0, 1 << 20) % (slack + 1)
    tallies = tallies.at[1:1 + 2 * pairs:2].set(giver - passed).at[2:2 + 2 * pairs:2].set(receiver + passed)
    return tallies[jax.random.permutation(jax.random.fold_in(own_key, 2), amount)]


def scatter_about(own_key, shape, deviation, reach, split=(), held_as=jnp.bfloat16):
    result = jax.random.normal(own_key, shape, jnp.float32) * deviation
    if len(split) > 0:
        result = level_of(own_key, shape, split, -0.22, 0.18) * result
    return jnp.clip(result, min=-reach, max=reach).astype(held_as)


def setup_inputs(seed: int = 0) -> dict:
    splits = jax.random.split(jax.random.key(seed), 7)
    queries = draw_queries(jax.random.fold_in(splits[6], 71), 0)
    resp_kv = scatter_about(splits[1], (TOKENS, KVH, 2 * HD), 1.0, 6.0, ((0, 32), (1, 8)))
    prompt_kv = draw_prompt_kv(jax.random.fold_in(splits[6], 71), 0)
    resp_prompt = plant(jax.random.randint(splits[3], (N_DP, RESP_DEV), 0, PROMPTS), jax.random.fold_in(splits[3], 1), 0, PROMPTS - 1).astype(jnp.int32)
    row_segment = jax.vmap(lambda own: jnp.searchsorted(jnp.cumsum(ragged_sizes(own, RESP_DEV, ROWS_DEV, ROWS_DEV // 2, 1)), jnp.arange(ROWS_DEV), side="right"))(jax.random.split(splits[4], N_DP)).reshape((N_DP, ROWS_DEV)).astype(jnp.int32)
    cotangent = scatter_about(splits[5], (TOKENS, HEADS * HD), 1.0, 6.0, ((0, 32), (1, 8)))
    return dict(queries=queries, resp_kv=resp_kv, prompt_kv=prompt_kv, resp_prompt=resp_prompt, row_segment=row_segment, cotangent=cotangent)


def block_attention(queries, resp_kv, prompt_all, resp_prompt, row_segment, cotangent, prompt_len):
    row_count = queries.shape[0]
    kv_groups = resp_kv.shape[1]
    head_width = resp_kv.shape[2] // 2
    grouped = queries.shape[1] // (kv_groups * head_width)
    score_scale = 1.0 / math.sqrt(head_width)
    window = row_count // 2
    q_heads = queries.reshape(row_count, kv_groups, grouped, head_width)
    g_heads = cotangent.reshape(row_count, kv_groups, grouped, head_width)
    resp_keys = resp_kv[..., :head_width]
    resp_vals = resp_kv[..., head_width:]
    position = jnp.arange(row_count, dtype=jnp.int32)
    self_mask = (row_segment[:, None] == row_segment[None, :]) & (position[None, :] <= position[:, None])
    self_scores = jnp.einsum('rkgd,jkd->kgrj', q_heads, resp_keys, preferred_element_type=jnp.float32) * score_scale
    self_scores = jnp.where(self_mask[None, None], self_scores, -1e+30)
    resp_count = resp_prompt.shape[0]
    seg_ids = jnp.arange(resp_count, dtype=jnp.int32)
    starts = lax.optimization_barrier(jnp.sum((row_segment[None, :] < seg_ids[:, None]).astype(jnp.int32), axis=1)).astype(jnp.int32)
    starts = jnp.minimum(starts, row_count - window).astype(jnp.int32)
    prompt_scores = []
    prompt_pieces = []
    full_max = lax.optimization_barrier(jnp.max(self_scores, axis=-1))
    for seg in range(resp_count):
        start = starts[seg]
        seg_window = lax.dynamic_slice_in_dim(row_segment, start, window, 0)
        live = seg_window == seg
        q_window = lax.dynamic_slice_in_dim(q_heads, start, window, 0)
        offset = (resp_prompt[seg] * prompt_len).astype(jnp.int32)
        piece = lax.dynamic_slice_in_dim(prompt_all, offset, prompt_len, 0)
        scores_now = jnp.einsum('rkgd,jkd->kgrj', q_window, piece[..., :head_width], preferred_element_type=jnp.float32) * score_scale
        scores_now = jnp.where(live[None, None, :, None], scores_now, -1e+30)
        window_max = lax.optimization_barrier(jnp.max(scores_now, axis=-1))
        placed_max = lax.dynamic_update_slice_in_dim(jnp.full(full_max.shape, -1e+30, jnp.float32), window_max, start, 2)
        placed_live = lax.dynamic_update_slice_in_dim(jnp.zeros((row_count,), jnp.bool_), live, start, 0)
        full_max = jnp.where(placed_live[None, None, :], jnp.maximum(full_max, placed_max), full_max)
        prompt_scores.append(scores_now)
        prompt_pieces.append((start, offset, q_window, piece))
    total = lax.optimization_barrier(jnp.sum(jnp.exp(self_scores - full_max[..., None]), axis=-1))
    for seg in range(resp_count):
        start = prompt_pieces[seg][0]
        max_window = lax.dynamic_slice_in_dim(full_max, start, window, 2)
        part_total = lax.optimization_barrier(jnp.sum(jnp.exp(prompt_scores[seg] - max_window[..., None]), axis=-1))
        total = total + lax.dynamic_update_slice_in_dim(jnp.zeros_like(total), part_total, start, 2)
    lse = full_max + jnp.log(total)
    self_probs = jnp.exp(self_scores - lse[..., None]).astype(jnp.bfloat16)
    out = jnp.einsum('kgrj,jkd->kgrd', self_probs, resp_vals, preferred_element_type=jnp.float32)
    prompt_probs = []
    for seg in range(resp_count):
        start, offset, q_window, piece = prompt_pieces[seg]
        lse_window = lax.dynamic_slice_in_dim(lse, start, window, 2)
        probs_now = jnp.exp(prompt_scores[seg] - lse_window[..., None]).astype(jnp.bfloat16)
        out_window = jnp.einsum('kgrj,jkd->kgrd', probs_now, piece[..., head_width:], preferred_element_type=jnp.float32)
        out = out + lax.dynamic_update_slice_in_dim(jnp.zeros_like(out), out_window, start, 2)
        prompt_probs.append(probs_now)
    attended = out.transpose(2, 0, 1, 3).reshape(row_count, -1)
    g_float = g_heads.astype(jnp.float32).transpose(1, 2, 0, 3)
    row_delta = lax.optimization_barrier(jnp.sum(g_float * out, axis=-1))
    self_dprob = jnp.einsum('rkgd,jkd->kgrj', g_heads, resp_vals, preferred_element_type=jnp.float32)
    self_dscore = (self_probs.astype(jnp.float32) * (self_dprob - row_delta[..., None]) * score_scale).astype(jnp.bfloat16)
    query_grad = jnp.einsum('kgrj,jkd->rkgd', self_dscore, resp_keys, preferred_element_type=jnp.float32)
    key_grad = jnp.einsum('kgrj,rkgd->jkd', self_dscore, q_heads, preferred_element_type=jnp.float32)
    value_grad = jnp.einsum('kgrj,rkgd->jkd', self_probs, g_heads, preferred_element_type=jnp.float32)
    prompt_grad = jnp.zeros(prompt_all.shape, jnp.float32)
    for seg in range(resp_count):
        start, offset, q_window, piece = prompt_pieces[seg]
        probs_now = prompt_probs[seg]
        g_window = lax.dynamic_slice_in_dim(g_heads, start, window, 0)
        delta_window = lax.dynamic_slice_in_dim(row_delta, start, window, 2)
        dprob_now = jnp.einsum('rkgd,jkd->kgrj', g_window, piece[..., head_width:], preferred_element_type=jnp.float32)
        dscore_now = (probs_now.astype(jnp.float32) * (dprob_now - delta_window[..., None]) * score_scale).astype(jnp.bfloat16)
        query_part = jnp.einsum('kgrj,jkd->rkgd', dscore_now, piece[..., :head_width], preferred_element_type=jnp.float32)
        query_grad = query_grad + lax.dynamic_update_slice_in_dim(jnp.zeros_like(query_grad), query_part, start, 0)
        key_part = jnp.einsum('kgrj,rkgd->jkd', dscore_now, q_window, preferred_element_type=jnp.float32)
        value_part = jnp.einsum('kgrj,rkgd->jkd', probs_now, g_window, preferred_element_type=jnp.float32)
        current = lax.dynamic_slice_in_dim(prompt_grad, offset, prompt_len, 0)
        prompt_grad = lax.dynamic_update_slice_in_dim(prompt_grad, current + jnp.concatenate([key_part, value_part], axis=-1), offset, 0)
    resp_grad = jnp.concatenate([key_grad, value_grad], axis=-1)
    return (attended, query_grad.reshape(row_count, -1), resp_grad, prompt_grad)

def reference(queries, resp_kv, prompt_kv, resp_prompt, row_segment, cotangent):

    def block_step(running, block_item):
        q_rows, kv_rows, prompts_here, segments_here, cot_rows = block_item
        attended, query_grad, resp_grad, prompt_grad = block_attention(q_rows, kv_rows, prompt_kv, prompts_here, segments_here, cot_rows, PLEN)
        return (running + prompt_grad, (attended.astype(jnp.bfloat16), query_grad.astype(jnp.bfloat16), resp_grad.astype(jnp.bfloat16)))
    block_items = (queries.reshape(N_DP, ROWS_DEV, -1), resp_kv.reshape(N_DP, ROWS_DEV, KVH, 2 * HD), resp_prompt, row_segment, cotangent.reshape(N_DP, ROWS_DEV, -1))
    summed, outputs = lax.scan(block_step, jnp.zeros(prompt_kv.shape, jnp.float32), block_items)
    attended, query_grad, resp_grad = outputs
    return (attended.reshape(TOKENS, -1), query_grad.reshape(TOKENS, -1), resp_grad.reshape(TOKENS, KVH, 2 * HD), summed)
```

```python
import math

import jax
import jax.numpy as jnp
from jax import lax
from jax.experimental import pallas as pl
from jax.experimental.pallas import tpu as pltpu
from jax.sharding import PartitionSpec as P

MESH = pl.DeviceIdType.MESH
HD = 128
NH = 8
ROWS = 128
WIN = 64
RESP = 4
WL = NH * WIN
NCH = 4
CK = 256
BLK = 64
SLAB = 32
OFFS = (0, 1, 7, 2, 6, 3, 5, 4)
SCALE = 1.0 / math.sqrt(HD)
ALPHA = SCALE * math.log2(math.e)
BF = jnp.bfloat16
F32 = jnp.float32


def dot(a, b):
    return jnp.dot(a, b, preferred_element_type=F32)


def dot_t(a, b):
    return lax.dot_general(a, b, (((1,), (1,)), ((), ())), preferred_element_type=F32)


class Work:
    def __init__(self, **refs):
        self.__dict__.update(refs)

    def prep(self):
        seg = self.seg[...].astype(F32)
        pos = lax.broadcasted_iota(jnp.int32, (1, ROWS), 1).astype(F32)
        for i in range(1, RESP):
            start = jnp.sum(jnp.where(seg < i, 1.0, 0.0), axis=1, keepdims=True)
            before = jnp.sum(jnp.where(seg < i - 1, 1.0, 0.0), axis=1, keepdims=True)
            pos = pos - jnp.where(seg >= i, start - before, 0.0)
        slot = seg * WIN + pos
        col = seg * (2 * WIN) + pos
        place = lax.broadcasted_iota(jnp.int32, (RESP * WIN, ROWS), 0).astype(F32)
        gather = jnp.where(place == slot, 1.0, 0.0).astype(BF)
        self.kvself[...] = dot(gather, self.rkv[...]).astype(BF)
        slot_t = jnp.broadcast_to(slot, (ROWS, ROWS)).T
        col_t = jnp.broadcast_to(col, (ROWS, ROWS)).T
        lane = lax.broadcasted_iota(jnp.int32, (ROWS, ROWS), 1).astype(F32)
        for i in range(RESP):
            here = lane + 128.0 * i
            self.spread[0:ROWS, i * 128 : (i + 1) * 128] = jnp.where(here == col_t, 1.0, 0.0).astype(BF)
            self.spread[ROWS : 2 * ROWS, i * 128 : (i + 1) * 128] = jnp.where(
                here == col_t + WIN, 1.0, 0.0
            ).astype(BF)
        for i in range(2):
            self.back[:, i * 128 : (i + 1) * 128] = jnp.where(lane + 128.0 * i == slot_t, 1.0, 0.0).astype(BF)
        spread = self.spread[...]
        for source, target in ((self.q, self.qt), (self.g, self.gt)):
            for pair in range(NH // 2):
                two = source[:, pair * 256 : (pair + 1) * 256]
                turned = jnp.concatenate([two[:, :HD].T, two[:, HD:].T], axis=1)
                placed = dot(turned, spread).astype(BF)
                for i in range(RESP):
                    target[i, :, pair * 128 : (pair + 1) * 128] = placed[:, i * 128 : (i + 1) * 128]

    def self_fwd(self):
        key = lax.broadcasted_iota(jnp.int32, (WIN, WL), 0)
        row = lax.broadcasted_iota(jnp.int32, (WIN, WL), 1) & (WIN - 1)
        seen = key <= row

        def body(i, carry):
            kv = self.kvself[pl.ds(pl.multiple_of(i * WIN, WIN), WIN), :]
            s = jnp.where(seen, dot(kv[:, :HD], self.qt[i]), -1e30)
            m = jnp.max(s, axis=0, keepdims=True)
            e = jnp.exp2((s - m) * ALPHA)
            eb = e.astype(BF)
            self.eself[i] = eb
            self.mself[i] = m
            self.accm[i] = m
            self.accl[i] = jnp.sum(e, axis=0, keepdims=True)
            self.acco[i] = dot(kv[:, HD:].T, eb)
            return carry

        lax.fori_loop(0, RESP, body, 0)

    def piece(self, j, i):
        p = self.rp[0, i]
        kv = self.kvb[j][lax.shift_right_logical(p, 1), pl.ds((p & 1) * 2, 2)]
        return kv.reshape(CK, 2 * HD)

    def fwd(self, j):
        def body(i, carry):
            kv = self.piece(j, i)
            s = dot(kv[:, :HD], self.qt[i])
            m = jnp.max(s, axis=0, keepdims=True)
            e = jnp.exp2((s - m) * ALPHA)
            eb = e.astype(BF)
            self.ebuf[j, i] = eb
            self.mbuf[j, i] = m
            total = jnp.sum(e, axis=0, keepdims=True)
            o = dot(kv[:, HD:].T, eb)
            old = self.accm[i]
            new = jnp.maximum(old, m)
            a = jnp.exp2((old - new) * ALPHA)
            b = jnp.exp2((m - new) * ALPHA)
            self.accm[i] = new
            self.accl[i] = self.accl[i] * a + total * b
            self.acco[i] = self.acco[i] * a + o * b
            return carry

        lax.fori_loop(0, RESP, body, 0)

    def middle(self):
        def body(i, carry):
            total = self.accl[i]
            self.lse[i] = self.accm[i] * ALPHA + jnp.log2(total)
            out = self.acco[i] * (1.0 / total)
            self.delta[i] = jnp.sum(self.gt[i].astype(F32) * out, axis=0, keepdims=True)
            self.outt[i] = out.astype(BF)
            return carry

        lax.fori_loop(0, RESP, body, 0)

    def grads(self, i, k, v, m, e):
        weight = e.astype(F32) * jnp.exp2(m * ALPHA - self.lse[i])
        wb = weight.astype(BF)
        ds = (weight * (dot(v, self.gt[i]) - self.delta[i])).astype(BF)
        dk = dot_t(ds, self.qt[i]) * SCALE
        dv = dot_t(wb, self.gt[i])
        dq = dot(k.T, ds)
        return jnp.concatenate([dk, dv], axis=1).astype(BF), dq

    def self_bwd(self):
        def body(i, carry):
            at = pl.ds(pl.multiple_of(i * WIN, WIN), WIN)
            kv = self.kvself[at, :]
            dkv, dq = self.grads(i, kv[:, :HD], kv[:, HD:], self.mself[i], self.eself[i])
            self.dself[at, :] = dkv
            self.dqt[i] = self.dqt[i] + dq
            return carry

        lax.fori_loop(0, RESP, body, 0)

    def bwd(self, j):
        def body(i, carry):
            kv = self.piece(j, i)
            dkv, dq = self.grads(i, kv[:, :HD], kv[:, HD:], self.mbuf[j, i], self.ebuf[j, i])
            self.dkv[j][i] = dkv.reshape(4, BLK, 2 * HD)
            if j == 0:
                self.dqt[i] = dq
            else:
                self.dqt[i] = self.dqt[i] + dq
            return carry

        lax.fori_loop(0, RESP, body, 0)

    def place_rows(self, source, scale, target):
        for head in range(NH):
            at = pl.ds((head // 2) * 128, 128)
            parts = [source[i, :, at] for i in range(RESP)]
            if scale is not None:
                parts = [part * scale for part in parts]
            whole = jnp.concatenate([part.astype(BF) for part in parts], axis=1)
            rows = self.spread[(head % 2) * ROWS : (head % 2 + 1) * ROWS, :]
            target[:, head * HD : (head + 1) * HD] = dot_t(rows, whole).astype(BF)

    def write_attended(self):
        self.place_rows(self.outt, None, self.attended)

    def write_query_grad(self):
        self.place_rows(self.dqt, SCALE, self.qgrad)

    def write_resp_grad(self):
        self.rgrad[...] = dot(self.back[...], self.dself[...]).astype(BF)

    def selected(self, j, p, part):
        total = None
        for i in range(RESP):
            mine = jnp.where(self.rp[0, i] == p, 1.0, 0.0)
            term = self.dkv[j][i, part].astype(F32) * mine
            total = term if total is None else total + term
        return total


WORK_SCRATCH = dict(
    kvself=pltpu.VMEM((RESP * WIN, 2 * HD), BF),
    spread=pltpu.VMEM((2 * ROWS, RESP * 128), BF),
    back=pltpu.VMEM((ROWS, RESP * WIN), BF),
    qt=pltpu.VMEM((RESP, HD, WL), BF),
    gt=pltpu.VMEM((RESP, HD, WL), BF),
    eself=pltpu.VMEM((RESP, WIN, WL), BF),
    ebuf=pltpu.VMEM((NCH, RESP, CK, WL), BF),
    mself=pltpu.VMEM((RESP, 1, WL), F32),
    mbuf=pltpu.VMEM((NCH, RESP, 1, WL), F32),
    accm=pltpu.VMEM((RESP, 1, WL), F32),
    accl=pltpu.VMEM((RESP, 1, WL), F32),
    lse=pltpu.VMEM((RESP, 1, WL), F32),
    delta=pltpu.VMEM((RESP, 1, WL), F32),
    acco=pltpu.VMEM((RESP, HD, WL), F32),
    outt=pltpu.VMEM((RESP, HD, WL), BF),
    dqt=pltpu.VMEM((RESP, HD, WL), F32),
    dself=pltpu.VMEM((RESP * WIN, 2 * HD), BF),
)


class Net:
    def __init__(self, send_sem, recv_sem):
        self.dp, self.t = lax.axis_index("dp"), lax.axis_index("tensor")
        self.x, self.y, self.c = self.dp // 8, (self.dp // 2) % 4, self.dp % 2
        self.send_sem, self.recv_sem = send_sem, recv_sem
        self.count = 0
        self.sent = []

    def device(self, x=None, y=None, c=None, t=None):
        x = self.x if x is None else x
        y = self.y if y is None else y
        c = self.c if c is None else c
        return (x * 8 + y * 2 + c, self.t if t is None else t)

    def along(self, axis, step):
        here = self.x if axis == "x" else self.y
        return self.device(**{axis: (here + step + 4) % 4})

    def copy(self, src, dst, device):
        index = self.count
        self.count += 1
        made = pltpu.make_async_remote_copy(
            src_ref=src,
            dst_ref=dst,
            send_sem=self.send_sem.at[index],
            recv_sem=self.recv_sem.at[index],
            device_id=device,
            device_id_type=MESH,
        )
        made.start()
        self.sent.append(made)
        return made

    def greet(self):
        barrier = pltpu.get_barrier_semaphore()
        partners = [self.along(axis, step) for axis in "xy" for step in (1, 3)]
        partners.append(self.device(c=1 - self.c))
        partners.extend(self.device(t=(self.t + step) % 8) for step in range(1, 8))
        for partner in partners:
            pl.semaphore_signal(barrier, inc=1, device_id=partner, device_id_type=MESH)
        pl.semaphore_wait(barrier, len(partners))

    def finish(self):
        for made in self.sent:
            made.wait_send()


class Gather:
    def __init__(self, net, j, buf):
        self.net, self.j, self.buf = net, j, buf

    def block(self, half, axis, at, first, size):
        rows = pl.ds(half * SLAB + first, size)
        net = self.net
        if axis == "x":
            return self.buf.at[at, slice(None), net.c, rows]
        return self.buf.at[slice(None), at, net.c, rows]

    def own(self, half, x, y, first, size):
        return self.buf.at[x, y, self.net.c, pl.ds(half * SLAB + first, size)]

    def start(self, arrived):
        net = self.net
        self.first = []
        for half in (0, 1):
            if arrived[half] is not None:
                arrived[half].wait_recv()
            axis = "xy"[half]
            mine = self.own(half, net.x, net.y, 0, SLAB)
            self.first.append([net.copy(mine, mine, net.along(axis, step)) for step in (1, 3)])

    def second(self):
        net = self.net
        self.onward = []
        for half in (0, 1):
            axis = "xy"[half]
            here = net.x if axis == "x" else net.y
            copies = []
            for way, step in enumerate((1, 3)):
                self.first[half][way].wait_recv()
                source = (here - step + 4) % 4
                x, y = (source, net.y) if axis == "x" else (net.x, source)
                part = self.own(half, x, y, way * (SLAB // 2), SLAB // 2)
                copies.append(net.copy(part, part, net.along(axis, step)))
            self.onward.append(copies)

    def third(self):
        net = self.net
        self.lines = []
        for half in (0, 1):
            for made in self.onward[half]:
                made.wait_recv()
            axis = "yx"[half]
            here = net.x if axis == "x" else net.y
            line = self.block(half, axis, here, 0, SLAB)
            self.lines.append([net.copy(line, line, net.along(axis, step)) for step in (1, 3)])

    def fourth(self):
        net = self.net
        self.last = []
        for half in (0, 1):
            axis = "yx"[half]
            here = net.x if axis == "x" else net.y
            for way, step in enumerate((1, 3)):
                self.lines[half][way].wait_recv()
                source = (here - step + 4) % 4
                part = self.block(half, axis, source, way * (SLAB // 2), SLAB // 2)
                self.last.append(net.copy(part, part, net.along(axis, step)))

    def across(self):
        net = self.net
        for made in self.last:
            made.wait_recv()
        mine = self.buf.at[:, :, net.c]
        self.sibling = net.copy(mine, mine, net.device(c=1 - net.c))

    def done(self):
        self.sibling.wait_recv()


class Scatter:
    def __init__(self, net, work, j, refs, out):
        self.net, self.work, self.j, self.out = net, work, j, out
        self.__dict__.update(refs)

    def start(self):
        net = self.net

        def body(p, carry):
            for half in (0, 1):
                value = self.work.selected(self.j, p, 2 * half + (1 - net.c))
                self.give[p // 2, (p % 2) * 2 + half] = value.astype(BF)
            return carry

        lax.fori_loop(0, 8, body, 0)
        self.sibling = net.copy(self.give, self.take, net.device(c=1 - net.c))

    def own(self):
        net = self.net
        self.sibling.wait_recv()

        def body(p, carry):
            for half in (0, 1):
                x, y = p // 2, (p % 2) * 2 + half
                value = self.work.selected(self.j, p, 2 * half + net.c) + self.take[x, y].astype(F32)
                self.held[x, y] = value.astype(BF)
            return carry

        lax.fori_loop(0, 8, body, 0)
        self.far = []
        for half in (0, 1):
            axis = "yx"[half]
            here = net.x if axis == "x" else net.y
            across = (here + 2) % 4
            copies = []
            for way, step in enumerate((1, 3)):
                rows = pl.ds(half * SLAB + way * (SLAB // 2), SLAB // 2)
                src = self.held.at[across, :, rows] if axis == "x" else self.held.at[:, across, rows]
                copies.append(net.copy(src, self.far1.at[half, way], net.along(axis, step)))
            self.far.append(copies)

    def line(self, half, axis, at):
        rows = pl.ds(half * SLAB, SLAB)
        return self.held[at, :, rows] if axis == "x" else self.held[:, at, rows]

    def near(self):
        net = self.net
        self.close = []
        for half in (0, 1):
            axis = "yx"[half]
            here = net.x if axis == "x" else net.y
            copies = []
            for way, step in enumerate((1, 3)):
                self.far[half][way].wait_recv()
                mine = self.line(half, axis, (here + step) % 4).astype(F32)
                more = self.far1[half, way].astype(F32)
                part = slice(way * (SLAB // 2), (way + 1) * (SLAB // 2))
                rest = slice((1 - way) * (SLAB // 2), (2 - way) * (SLAB // 2))
                self.near1[half, way, :, part] = (mine[:, part] + more).astype(BF)
                self.near1[half, way, :, rest] = mine[:, rest].astype(BF)
                copies.append(net.copy(self.near1.at[half, way], self.near2.at[half, way], net.along(axis, step)))
            self.close.append(copies)

    def turn(self):
        net = self.net
        self.far = []
        for half in (0, 1):
            axis = "yx"[half]
            here = net.x if axis == "x" else net.y
            total = self.line(half, axis, here).astype(F32)
            for way in (0, 1):
                self.close[half][way].wait_recv()
                total = total + self.near2[half, way].astype(F32)
            self.rest[half] = total.astype(BF)
            axis = "xy"[half]
            here = net.x if axis == "x" else net.y
            copies = []
            for way, step in enumerate((1, 3)):
                src = self.rest.at[half, (here + 2) % 4, pl.ds(way * (SLAB // 2), SLAB // 2)]
                copies.append(net.copy(src, self.far2.at[half, way], net.along(axis, step)))
            self.far.append(copies)

    def near_again(self):
        net = self.net
        self.close = []
        for half in (0, 1):
            axis = "xy"[half]
            here = net.x if axis == "x" else net.y
            copies = []
            for way, step in enumerate((1, 3)):
                self.far[half][way].wait_recv()
                mine = self.rest[half, (here + step) % 4].astype(F32)
                more = self.far2[half, way].astype(F32)
                part = slice(way * (SLAB // 2), (way + 1) * (SLAB // 2))
                rest = slice((1 - way) * (SLAB // 2), (2 - way) * (SLAB // 2))
                self.near3[half, way, part] = (mine[part] + more).astype(BF)
                self.near3[half, way, rest] = mine[rest].astype(BF)
                copies.append(net.copy(self.near3.at[half, way], self.near4.at[half, way], net.along(axis, step)))
            self.close.append(copies)

    def home(self):
        net = self.net
        self.back = []
        for half in (0, 1):
            axis = "xy"[half]
            here = net.x if axis == "x" else net.y
            total = self.rest[half, here].astype(F32)
            for way in (0, 1):
                self.close[half][way].wait_recv()
                total = total + self.near4[half, way].astype(F32)
            away = OFFS[2 * self.j + half]
            if away == 0:
                self.out[net.t] = total.astype(BF)
            else:
                self.ready[half] = total.astype(BF)
                self.back.append(
                    net.copy(self.ready.at[half], self.out.at[net.t], net.device(t=(net.t + away) % 8))
                )

    def done(self):
        for made in self.back:
            made.wait_recv()


SCATTER_SCRATCH = dict(
    give=pltpu.VMEM((4, 4, BLK, 2 * HD), BF),
    take=pltpu.VMEM((4, 4, BLK, 2 * HD), BF),
    held=pltpu.VMEM((4, 4, BLK, 2 * HD), BF),
    far1=pltpu.VMEM((2, 2, 4, SLAB // 2, 2 * HD), BF),
    near1=pltpu.VMEM((2, 2, 4, SLAB, 2 * HD), BF),
    near2=pltpu.VMEM((2, 2, 4, SLAB, 2 * HD), BF),
    rest=pltpu.VMEM((2, 4, SLAB, 2 * HD), BF),
    far2=pltpu.VMEM((2, 2, SLAB // 2, 2 * HD), BF),
    near3=pltpu.VMEM((2, 2, SLAB, 2 * HD), BF),
    near4=pltpu.VMEM((2, 2, SLAB, 2 * HD), BF),
    ready=pltpu.VMEM((2, SLAB, 2 * HD), BF),
)
COPIES = 7 + NCH * (4 + 4 + 4 + 4 + 1) + NCH * (1 + 4 + 4 + 4 + 4) + 7
SCRATCH = (
    [("send_sem", pltpu.SemaphoreType.DMA((COPIES,))), ("recv_sem", pltpu.SemaphoreType.DMA((COPIES,)))]
    + [("kvb", pltpu.VMEM((4, 4, 2, BLK, 2 * HD), BF))] * NCH
    + [("dkv", pltpu.VMEM((RESP, 4, BLK, 2 * HD), BF))] * NCH
    + list(WORK_SCRATCH.items())
    + list(SCATTER_SCRATCH.items()) * NCH
)


def kernel(q, g, rkv, slabs, seg, rp, attended, qgrad, rgrad, pgrad, *scratch):
    named = {}
    for (name, _), ref in zip(SCRATCH, scratch):
        named.setdefault(name, []).append(ref)
    refs = {name: named[name][0] for name in WORK_SCRATCH}
    work = Work(
        q=q, g=g, rkv=rkv, seg=seg, rp=rp, kvb=named["kvb"], dkv=named["dkv"],
        attended=attended, qgrad=qgrad, rgrad=rgrad, **refs
    )
    net = Net(named["send_sem"][0], named["recv_sem"][0])
    gathers = [Gather(net, j, named["kvb"][j]) for j in range(NCH)]
    scatters = [
        Scatter(net, work, j, {name: named[name][j] for name in SCATTER_SCRATCH}, pgrad) for j in range(NCH)
    ]
    net.greet()
    arrivals = [None]
    for place in range(1, 8):
        to = (net.t - OFFS[place] + 8) % 8
        target = gathers[place // 2].own(place % 2, net.x, net.y, 0, SLAB)
        arrivals.append(net.copy(slabs.at[to], target, net.device(t=to)))
    gathers[0].buf[net.x, net.y, net.c, 0:SLAB] = slabs[net.t]
    for j in range(NCH):
        gathers[j].start(arrivals[2 * j : 2 * j + 2])
    work.prep()
    for j in range(NCH):
        gathers[j].second()
    work.self_fwd()
    gathers[0].third()
    gathers[1].third()
    gathers[0].fourth()
    gathers[2].third()
    gathers[0].across()
    gathers[1].fourth()
    gathers[3].third()
    gathers[0].done()
    work.fwd(0)
    gathers[1].across()
    gathers[2].fourth()
    gathers[1].done()
    work.fwd(1)
    gathers[2].across()
    gathers[3].fourth()
    gathers[2].done()
    work.fwd(2)
    gathers[3].across()
    gathers[3].done()
    work.fwd(3)
    work.middle()
    stages = ("start", "own", "near", "turn", "near_again", "home")
    for turn in range(NCH + len(stages) - 1):
        if turn < NCH:
            work.bwd(turn)
        for late in range(len(stages) - 1, -1, -1):
            if 0 <= turn - late < NCH:
                getattr(scatters[turn - late], stages[late])()
        if turn == NCH:
            work.write_attended()
        if turn == NCH + 1:
            work.self_bwd()
            work.write_resp_grad()
        if turn == NCH + 2:
            work.write_query_grad()
    for scatter in scatters:
        scatter.done()
    net.finish()


def local(queries, resp_kv, prompt_kv, resp_prompt, row_segment, cotangent):
    vmem = pl.BlockSpec(memory_space=pltpu.VMEM)
    slabs = prompt_kv.transpose(1, 0, 2)
    attended, query_grad, resp_grad, prompt_grad = pl.pallas_call(
        kernel,
        out_shape=(
            jax.ShapeDtypeStruct((ROWS, NH * HD), BF),
            jax.ShapeDtypeStruct((ROWS, NH * HD), BF),
            jax.ShapeDtypeStruct((ROWS, 2 * HD), BF),
            jax.ShapeDtypeStruct((8, SLAB, 2 * HD), BF),
        ),
        in_specs=[vmem] * 5 + [pl.BlockSpec(memory_space=pltpu.SMEM)],
        out_specs=[vmem] * 4,
        scratch_shapes=[shape for _, shape in SCRATCH],
        compiler_params=pltpu.CompilerParams(
            collective_id=0, has_side_effects=True, vmem_limit_bytes=56 << 20
        ),
    )(queries, cotangent, resp_kv[:, 0], slabs, row_segment, resp_prompt)
    return attended, query_grad, resp_grad[:, None], prompt_grad.transpose(1, 0, 2).astype(F32)


def solution(mesh):
    return jax.shard_map(
        local,
        mesh=mesh,
        in_specs=(
            P("dp", "tensor"),
            P("dp", "tensor", None),
            P(("dp", "tensor"), None, None),
            P("dp", None),
            P("dp", None),
            P("dp", "tensor"),
        ),
        out_specs=(
            P("dp", "tensor"),
            P("dp", "tensor"),
            P("dp", "tensor", None),
            P(("dp", "tensor"), None, None),
        ),
        check_vma=False,
    )
```

```python
import math

import jax
import jax.numpy as jnp
from jax import lax
from jax.experimental import pallas as pl
from jax.experimental.pallas import tpu as pltpu
from jax.sharding import PartitionSpec as P

MESH = pl.DeviceIdType.MESH
HD = 128
NH = 8
ROWS = 128
WIN = 64
RESP = 4
WL = NH * WIN
NCH = 4
CK = 256
BLK = 64
SLAB = 32
OFFS = (0, 1, 7, 2, 6, 3, 5, 4)
GATHER_MERGED = (1, 2)
GATHER_RELAYED = (0, 1, 2, 3)
SCATTER_RELAYED = ()
SCATTER_MERGED = (1,)
SCALE = 1.0 / math.sqrt(HD)
ALPHA = SCALE * math.log2(math.e)
BF = jnp.bfloat16
F32 = jnp.float32


def dot(a, b):
    return jnp.dot(a, b, preferred_element_type=F32)


def dot_t(a, b):
    return lax.dot_general(a, b, (((1,), (1,)), ((), ())), preferred_element_type=F32)


class Work:
    def __init__(self, **refs):
        self.__dict__.update(refs)

    def prep(self):
        seg = self.seg[...].astype(F32)
        pos = lax.broadcasted_iota(jnp.int32, (1, ROWS), 1).astype(F32)
        for i in range(1, RESP):
            start = jnp.sum(jnp.where(seg < i, 1.0, 0.0), axis=1, keepdims=True)
            before = jnp.sum(jnp.where(seg < i - 1, 1.0, 0.0), axis=1, keepdims=True)
            pos = pos - jnp.where(seg >= i, start - before, 0.0)
        slot = seg * WIN + pos
        col = seg * (2 * WIN) + pos
        place = lax.broadcasted_iota(jnp.int32, (RESP * WIN, ROWS), 0).astype(F32)
        gather = jnp.where(place == slot, 1.0, 0.0).astype(BF)
        self.kvself[...] = dot(gather, self.rkv[...]).astype(BF)
        slot_t = jnp.broadcast_to(slot, (ROWS, ROWS)).T
        col_t = jnp.broadcast_to(col, (ROWS, ROWS)).T
        lane = lax.broadcasted_iota(jnp.int32, (ROWS, ROWS), 1).astype(F32)
        for i in range(RESP):
            here = lane + 128.0 * i
            self.spread[0:ROWS, i * 128 : (i + 1) * 128] = jnp.where(here == col_t, 1.0, 0.0).astype(BF)
            self.spread[ROWS : 2 * ROWS, i * 128 : (i + 1) * 128] = jnp.where(
                here == col_t + WIN, 1.0, 0.0
            ).astype(BF)
        for i in range(2):
            self.back[:, i * 128 : (i + 1) * 128] = jnp.where(lane + 128.0 * i == slot_t, 1.0, 0.0).astype(BF)
        spread = self.spread[...]
        for source, target in ((self.q, self.qt), (self.g, self.gt)):
            for pair in range(NH // 2):
                two = source[:, pair * 256 : (pair + 1) * 256]
                turned = jnp.concatenate([two[:, :HD].T, two[:, HD:].T], axis=1)
                placed = dot(turned, spread).astype(BF)
                for i in range(RESP):
                    target[i, :, pair * 128 : (pair + 1) * 128] = placed[:, i * 128 : (i + 1) * 128]

    def self_fwd(self):
        key = lax.broadcasted_iota(jnp.int32, (WIN, WL), 0)
        row = lax.broadcasted_iota(jnp.int32, (WIN, WL), 1) & (WIN - 1)
        seen = key <= row

        def body(i, carry):
            k = self.kvself[pl.ds(pl.multiple_of(i * WIN, WIN), WIN), 0:HD]
            s = jnp.where(seen, dot(k, self.qt[i]), -1e30)
            m = jnp.max(s, axis=0, keepdims=True)
            e = jnp.exp2((s - m) * ALPHA)
            self.wself[i] = e.astype(BF)
            self.mself[i] = m
            self.accm[i] = m
            self.accl[i] = jnp.sum(e, axis=0, keepdims=True)
            return carry

        lax.fori_loop(0, RESP, body, 0, unroll=True)

    def piece(self, bufs, j, i):
        p = self.rp[0, i]
        return bufs[j][lax.shift_right_logical(p, 1), pl.ds((p & 1) * 2, 2)].reshape(CK, HD)

    def fwd(self, j):
        def body(i, carry):
            s = dot(self.piece(self.kb, j, i), self.qt[i])
            m = jnp.max(s, axis=0, keepdims=True)
            e = jnp.exp2((s - m) * ALPHA)
            self.weight[j, i] = e.astype(BF)
            self.mbuf[j, i] = m
            old = self.accm[i]
            new = jnp.maximum(old, m)
            self.accl[i] = self.accl[i] * jnp.exp2((old - new) * ALPHA) + jnp.sum(
                e, axis=0, keepdims=True
            ) * jnp.exp2((m - new) * ALPHA)
            self.accm[i] = new
            return carry

        lax.fori_loop(0, RESP, body, 0, unroll=True)

    def middle(self):
        def body(i, carry):
            lse = self.accm[i] * ALPHA + jnp.log2(self.accl[i])
            self.lse[i] = lse
            weight = (self.wself[i].astype(F32) * jnp.exp2(self.mself[i] * ALPHA - lse)).astype(BF)
            self.wself[i] = weight
            v = self.kvself[pl.ds(pl.multiple_of(i * WIN, WIN), WIN), HD : 2 * HD]
            self.acco[i] = dot(v.T, weight)
            return carry

        lax.fori_loop(0, RESP, body, 0, unroll=True)

    def gradv(self, j):
        def body(i, carry):
            weight = self.weight[j, i].astype(F32) * jnp.exp2(self.mbuf[j, i] * ALPHA - self.lse[i])
            weight = weight.astype(BF)
            self.weight[j, i] = weight
            self.grads["v"][j][i] = dot_t(weight, self.gt[i]).astype(BF).reshape(4, BLK, HD)
            return carry

        lax.fori_loop(0, RESP, body, 0, unroll=True)

    def out(self, j):
        def body(i, carry):
            self.acco[i] = self.acco[i] + dot(self.piece(self.vb, j, i).T, self.weight[j, i])
            return carry

        lax.fori_loop(0, RESP, body, 0, unroll=True)

    def deltas(self):
        def body(i, carry):
            out = self.acco[i]
            self.delta[i] = jnp.sum(self.gt[i].astype(F32) * out, axis=0, keepdims=True)
            self.outt[i] = out.astype(BF)
            return carry

        lax.fori_loop(0, RESP, body, 0, unroll=True)

    def dscore(self, i, v, weight):
        return (weight.astype(F32) * (dot(v, self.gt[i]) - self.delta[i])).astype(BF)

    def self_bwd(self):
        def body(i, carry):
            at = pl.ds(pl.multiple_of(i * WIN, WIN), WIN)
            kv = self.kvself[at, :]
            ds = self.dscore(i, kv[:, HD:], self.wself[i])
            dk = dot_t(ds, self.qt[i]) * SCALE
            dv = dot_t(self.wself[i], self.gt[i])
            self.dself[at, :] = jnp.concatenate([dk, dv], axis=1).astype(BF)
            self.dqt[i] = dot(kv[:, :HD].T, ds)
            return carry

        lax.fori_loop(0, RESP, body, 0, unroll=True)

    def bwd(self, j):
        def body(i, carry):
            ds = self.dscore(i, self.piece(self.vb, j, i), self.weight[j, i])
            self.grads["k"][j][i] = (dot_t(ds, self.qt[i]) * SCALE).astype(BF).reshape(4, BLK, HD)
            self.weight[j, i] = ds
            return carry

        lax.fori_loop(0, RESP, body, 0, unroll=True)

    def gradq(self):
        def body(i, carry):
            total = self.dqt[i]
            for j in range(NCH):
                total = total + dot(self.piece(self.kb, j, i).T, self.weight[j, i])
            self.dqt[i] = total
            return carry

        lax.fori_loop(0, RESP, body, 0, unroll=True)

    def place_rows(self, source, scale, target):
        for head in range(NH):
            at = pl.ds((head // 2) * 128, 128)
            parts = [source[i, :, at] for i in range(RESP)]
            if scale is not None:
                parts = [part * scale for part in parts]
            whole = jnp.concatenate([part.astype(BF) for part in parts], axis=1)
            rows = self.spread[(head % 2) * ROWS : (head % 2 + 1) * ROWS, :]
            target[:, head * HD : (head + 1) * HD] = dot_t(rows, whole).astype(BF)

    def write_attended(self):
        self.place_rows(self.outt, None, self.attended)

    def write_query_grad(self):
        self.place_rows(self.dqt, SCALE, self.qgrad)

    def write_resp_grad(self):
        self.rgrad[...] = dot(self.back[...], self.dself[...]).astype(BF)

    def selected(self, kind, j, p, part):
        total = None
        for i in range(RESP):
            mine = jnp.where(self.rp[0, i] == p, 1.0, 0.0).astype(BF)
            term = self.grads[kind][j][i, part] * mine
            total = term if total is None else total + term
        return total


WORK_SCRATCH = dict(
    kvself=pltpu.VMEM((RESP * WIN, 2 * HD), BF),
    spread=pltpu.VMEM((2 * ROWS, RESP * 128), BF),
    back=pltpu.VMEM((ROWS, RESP * WIN), BF),
    qt=pltpu.VMEM((RESP, HD, WL), BF),
    gt=pltpu.VMEM((RESP, HD, WL), BF),
    wself=pltpu.VMEM((RESP, WIN, WL), BF),
    weight=pltpu.VMEM((NCH, RESP, CK, WL), BF),
    mself=pltpu.VMEM((RESP, 1, WL), F32),
    mbuf=pltpu.VMEM((NCH, RESP, 1, WL), F32),
    accm=pltpu.VMEM((RESP, 1, WL), F32),
    accl=pltpu.VMEM((RESP, 1, WL), F32),
    lse=pltpu.VMEM((RESP, 1, WL), F32),
    delta=pltpu.VMEM((RESP, 1, WL), F32),
    acco=pltpu.VMEM((RESP, HD, WL), F32),
    outt=pltpu.VMEM((RESP, HD, WL), BF),
    dqt=pltpu.VMEM((RESP, HD, WL), F32),
    dself=pltpu.VMEM((RESP * WIN, 2 * HD), BF),
)


class Net:
    def __init__(self, send_sem, recv_sem):
        self.dp, self.t = lax.axis_index("dp"), lax.axis_index("tensor")
        self.x, self.y, self.c = self.dp // 8, (self.dp // 2) % 4, self.dp % 2
        self.send_sem, self.recv_sem = send_sem, recv_sem
        self.count = 0
        self.sent = []

    def at(self, axis):
        return self.x if axis == "x" else self.y

    def device(self, axis=None, step=0, up=0, other=False):
        x = (self.x + step) % 4 if axis == "x" else self.x
        y = (self.y + step) % 4 if axis == "y" else self.y
        c = 1 - self.c if other else self.c
        return (x * 8 + y * 2 + c, (self.t + up) % 8)

    def copy(self, src, dst, device):
        index = self.count
        self.count += 1
        if index >= SENDS:
            self.sent[index - SENDS].wait_send()
        made = pltpu.make_async_remote_copy(
            src_ref=src,
            dst_ref=dst,
            send_sem=self.send_sem.at[index % SENDS],
            recv_sem=self.recv_sem.at[index],
            device_id=device,
            device_id_type=MESH,
        )
        made.start()
        self.sent.append(made)
        return made

    def greet(self, targets):
        barrier = pltpu.get_barrier_semaphore()
        for axis, step, up, other in targets:
            pl.semaphore_signal(
                barrier, inc=1, device_id=self.device(axis, 4 - step, 8 - up, other), device_id_type=MESH
            )

    def greeted(self, targets):
        pl.semaphore_wait(pltpu.get_barrier_semaphore(), len(targets))

    def finish(self):
        for made in self.sent[-SENDS:]:
            made.wait_send()


def first_axis(place):
    return "xy"[place % 2]


def second_axis(place):
    return "yx"[place % 2]


def targets():
    found = {(None, 0, 0, True)}
    for axis in "xy":
        found.update((axis, step, 0, False) for step in (1, 2, 3))
    for place in range(1, 8):
        for merged, up in ((GATHER_MERGED, -OFFS[place] % 8), (SCATTER_MERGED, OFFS[place])):
            found.add((None, 0, up, False))
            if place in merged:
                found.update((first_axis(place), step, up, False) for step in (1, 2, 3))
    return sorted(found, key=str)


class Gather:
    def __init__(self, net, place, buf):
        self.net, self.place, self.buf = net, place, buf
        self.low = (place % 2) * SLAB

    def line(self, axis, at, low=0, size=SLAB):
        rows = pl.ds(self.low + low, size)
        if axis == "x":
            return self.buf.at[at, :, self.net.c, rows]
        return self.buf.at[:, at, self.net.c, rows]

    def mine(self):
        net = self.net
        return self.buf.at[net.x, net.y, net.c, pl.ds(self.low, SLAB)]

    def up(self, slabs):
        net, place, axis = self.net, self.place, first_axis(self.place)
        away = -OFFS[place] % 8
        slab = slabs.at[(net.t + away) % 8]
        self.arrived, self.lined = None, []
        if place == 0:
            self.buf[net.x, net.y, net.c, 0:SLAB] = slab[...]
            self.lined = [net.copy(slab, self.mine(), net.device(axis, step)) for step in (1, 2, 3)]
        elif place in GATHER_MERGED:
            self.lined = [net.copy(slab, self.mine(), net.device(axis, step, away)) for step in (1, 2, 3, 0)]
        else:
            self.arrived = net.copy(slab, self.mine(), net.device(None, 0, away))

    def first(self):
        if self.arrived is not None:
            net, axis = self.net, first_axis(self.place)
            self.arrived.wait_recv()
            self.lined = [net.copy(self.mine(), self.mine(), net.device(axis, step)) for step in (1, 2, 3)]

    def second(self):
        net, axis = self.net, second_axis(self.place)
        for made in self.lined:
            made.wait_recv()
        whole = self.line(axis, net.at(axis))
        steps = (1, 3) if self.place in GATHER_RELAYED else (1, 2, 3)
        self.lines = [net.copy(whole, whole, net.device(axis, step)) for step in steps]

    def relay(self):
        if self.place in GATHER_RELAYED:
            net, axis = self.net, second_axis(self.place)
            handed = []
            for way, step in enumerate((1, 3)):
                self.lines[way].wait_recv()
                part = self.line(axis, (net.at(axis) + 4 - step) % 4, way * (SLAB // 2), SLAB // 2)
                handed.append(net.copy(part, part, net.device(axis, step)))
            self.lines = handed

    def across(self):
        net = self.net
        for made in self.lines:
            made.wait_recv()
        held = self.buf.at[:, :, net.c, pl.ds(self.low, SLAB)]
        self.sibling = net.copy(held, held, net.device(other=True))

    def done(self):
        self.sibling.wait_recv()


class Scatter:
    def __init__(self, net, work, kind, j, refs, final, heads):
        self.net, self.work, self.kind, self.j, self.final, self.heads = net, work, kind, j, final, heads
        self.relayed = f"{kind}{j}" in SCATTER_RELAYED
        self.__dict__.update(refs)

    def start(self):
        net = self.net

        def body(p, carry):
            for half in (0, 1):
                value = self.work.selected(self.kind, self.j, p, 2 * half + (1 - net.c))
                self.give[p // 2, (p % 2) * 2 + half] = value
            return carry

        lax.fori_loop(0, 8, body, 0, unroll=4)
        self.sibling = net.copy(self.give, self.take, net.device(other=True))

    def line(self, half, axis, at, low=0, size=SLAB):
        rows = pl.ds(half * SLAB + low, size)
        return self.held.at[at, :, rows] if axis == "x" else self.held.at[:, at, rows]

    def own(self):
        net = self.net
        self.sibling.wait_recv()

        def body(p, carry):
            for half in (0, 1):
                x, y = p // 2, (p % 2) * 2 + half
                value = self.work.selected(self.kind, self.j, p, 2 * half + net.c)
                self.held[x, y] = (value.astype(F32) + self.take[x, y].astype(F32)).astype(BF)
            return carry

        lax.fori_loop(0, 8, body, 0, unroll=4)
        self.lined = []
        for half in (0, 1):
            axis = second_axis(half)
            if self.relayed:
                copies = []
                for way, step in enumerate((1, 3)):
                    part = pl.ds(way * (SLAB // 2), SLAB // 2)
                    src = self.line(half, axis, (net.at(axis) + 2) % 4, way * (SLAB // 2), SLAB // 2)
                    copies.append(net.copy(src, self.came.at[half, 2, :, part], net.device(axis, step)))
                self.lined.append(copies)
                continue
            self.lined.append(
                [
                    net.copy(
                        self.line(half, axis, (net.at(axis) + step) % 4),
                        self.came.at[half, step - 1],
                        net.device(axis, step),
                    )
                    for step in (1, 2, 3)
                ]
            )

    def near(self):
        if self.relayed:
            net = self.net
            far, self.lined = self.lined, []
            for half in (0, 1):
                axis = second_axis(half)
                copies = []
                for way, step in enumerate((1, 3)):
                    far[half][way].wait_recv()
                    mine = self.line(half, axis, (net.at(axis) + step) % 4)[...]
                    part = slice(way * (SLAB // 2), (way + 1) * (SLAB // 2))
                    rest = slice((1 - way) * (SLAB // 2), (2 - way) * (SLAB // 2))
                    added = mine[:, part].astype(F32) + self.came[half, 2, :, part].astype(F32)
                    self.handed[half, way, :, part] = added.astype(BF)
                    self.handed[half, way, :, rest] = mine[:, rest]
                    copies.append(
                        net.copy(self.handed.at[half, way], self.came.at[half, way], net.device(axis, step))
                    )
                self.lined.append(copies)

    def turn(self):
        net = self.net
        self.homeward = []
        for half in (0, 1):
            axis = second_axis(half)
            total = self.line(half, axis, net.at(axis))[...].astype(F32)
            for index, made in enumerate(self.lined[half]):
                made.wait_recv()
                total = total + self.came[half, index].astype(F32)
            self.rest[half] = total.astype(BF)
            place, axis = 2 * self.j + half, first_axis(half)
            away = OFFS[place] if place in SCATTER_MERGED else 0
            copies = []
            for step in (1, 2, 3, 0):
                src, dst = self.rest.at[half, (net.at(axis) + step) % 4], self.final.at[place, step]
                if away == 0 and step == 0:
                    self.final[place, 0] = src[...]
                else:
                    copies.append(net.copy(src, dst, net.device(axis, step, away)))
            self.homeward.append(copies)

    def summed(self, place, half):
        for made in self.homeward[half]:
            made.wait_recv()
        total = self.final[place, 0].astype(F32)
        for step in (1, 2, 3):
            total = total + self.final[place, step].astype(F32)
        return total

    def up(self):
        net = self.net
        self.last = [None, None]
        for half in (0, 1):
            place = 2 * self.j + half
            if OFFS[place] != 0 and place not in SCATTER_MERGED:
                self.ready[half] = self.summed(place, half).astype(BF)
                self.last[half] = net.copy(
                    self.ready.at[half], self.came_up.at[half], net.device(None, 0, OFFS[place])
                )

    def sum(self):
        net = self.net
        for half in (0, 1):
            place = 2 * self.j + half
            head = (net.t + 8 - OFFS[place]) % 8
            lanes = slice(0, HD) if self.kind == "k" else slice(HD, 2 * HD)
            if self.last[half] is None:
                self.heads[head, :, lanes] = self.summed(place, half)
            else:
                self.last[half].wait_recv()
                self.heads[head, :, lanes] = self.came_up[half].astype(F32)


SCATTER_SCRATCH = dict(
    give=pltpu.VMEM((4, 4, BLK, HD), BF),
    take=pltpu.VMEM((4, 4, BLK, HD), BF),
    held=pltpu.VMEM((4, 4, BLK, HD), BF),
    came=pltpu.VMEM((2, 3, 4, SLAB, HD), BF),
    handed=pltpu.VMEM((2, 2, 4, SLAB, HD), BF),
    rest=pltpu.VMEM((2, 4, SLAB, HD), BF),
    ready=pltpu.VMEM((2, SLAB, HD), BF),
    came_up=pltpu.VMEM((2, SLAB, HD), BF),
)
COPIES = 252
SENDS = 64
SCRATCH = (
    [("send_sem", pltpu.SemaphoreType.DMA((SENDS,))), ("recv_sem", pltpu.SemaphoreType.DMA((COPIES,)))]
    + [("kb", pltpu.VMEM((4, 4, 2, BLK, HD), BF)), ("vb", pltpu.VMEM((4, 4, 2, BLK, HD), BF))] * NCH
    + [("dk", pltpu.VMEM((RESP, 4, BLK, HD), BF)), ("dv", pltpu.VMEM((RESP, 4, BLK, HD), BF))] * NCH
    + [
        ("kslabs", pltpu.VMEM((8, SLAB, HD), BF)),
        ("vslabs", pltpu.VMEM((8, SLAB, HD), BF)),
        ("wide", pltpu.VMEM((2, SLAB * 8, HD), F32)),
        ("final", pltpu.VMEM((8, 4, SLAB, HD), BF)),
        ("final", pltpu.VMEM((8, 4, SLAB, HD), BF)),
        ("near_sem", pltpu.SemaphoreType.DMA((9,))),
        ("q", pltpu.VMEM((ROWS, NH * HD), BF)),
        ("g", pltpu.VMEM((ROWS, NH * HD), BF)),
        ("rkv", pltpu.VMEM((ROWS, 2 * HD), BF)),
        ("pkv", pltpu.VMEM((SLAB, 8, 2 * HD), BF)),
        ("seg", pltpu.VMEM((1, ROWS), jnp.int32)),
        ("attended", pltpu.VMEM((ROWS, NH * HD), BF)),
        ("qgrad", pltpu.VMEM((ROWS, NH * HD), BF)),
        ("rgrad", pltpu.VMEM((ROWS, 2 * HD), BF)),
        ("heads", pltpu.VMEM((8, SLAB, 2 * HD), F32)),
        ("pgrad", pltpu.VMEM((SLAB, 8, 2 * HD), F32)),
    ]
    + list(WORK_SCRATCH.items())
    + list(SCATTER_SCRATCH.items()) * (2 * NCH)
)


INPUTS = ("pkv", "q", "g", "rkv", "seg")
OUTPUTS = ("attended", "qgrad", "rgrad", "pgrad")


def kernel(q, g, rkv, pkv, seg, rp, attended, qgrad, rgrad, pgrad, *scratch):
    outer = dict(q=q, g=g, rkv=rkv, pkv=pkv, seg=seg, attended=attended, qgrad=qgrad, rgrad=rgrad, pgrad=pgrad)
    named = {}
    for (name, _), ref in zip(SCRATCH, scratch):
        named.setdefault(name, []).append(ref)
    inner = {name: named[name][0] for name in outer}
    refs = {name: named[name][0] for name in WORK_SCRATCH}
    work = Work(rp=rp, kb=named["kb"], vb=named["vb"], grads=dict(k=named["dk"], v=named["dv"]), **inner, **refs)
    near_sem = named["near_sem"][0]
    moves = {}
    for index, name in enumerate(INPUTS):
        moves[name] = pltpu.make_async_copy(outer[name], inner[name], near_sem.at[index])
    for index, name in enumerate(OUTPUTS):
        moves[name] = pltpu.make_async_copy(inner[name], outer[name], near_sem.at[len(INPUTS) + index])
    moves["pkv"].start()
    net = Net(named["send_sem"][0], named["recv_sem"][0])
    slabs = dict(k=named["kslabs"][0], v=named["vslabs"][0])
    wide, heads = named["wide"][0], named["heads"][0]
    gk = [Gather(net, place, named["kb"][place // 2]) for place in range(8)]
    gv = [Gather(net, place, named["vb"][place // 2]) for place in range(8)]
    scatters = []
    for index in range(2 * NCH):
        scratch_of = {name: named[name][index] for name in SCATTER_SCRATCH}
        kind, j = "kv"[index // NCH], index % NCH
        scatters.append(Scatter(net, work, kind, j, scratch_of, named["final"][index // NCH], heads))
    sk, sv = scatters[:NCH], scatters[NCH:]
    net.greet(targets())
    for name in INPUTS[1:]:
        moves[name].start()
    moves["pkv"].wait()
    pkv = inner["pkv"]
    for part in (0, 1):
        wide[part] = pkv[:, :, part * HD : (part + 1) * HD].astype(F32).reshape(SLAB * 8, HD)
    for head in range(8):
        for part in (0, 1):
            slabs["kv"[part]][head] = wide[part, pl.ds(head, SLAB, stride=8), :].astype(BF)
    net.greeted(targets())
    for gather in gk:
        gather.up(slabs["k"])
    for gather in gv:
        gather.up(slabs["v"])
    for name in INPUTS[1:]:
        moves[name].wait()
    work.prep()
    work.self_fwd()
    gk[0].second()
    gv[0].second()
    gk[1].second()
    gk[3].first()
    gk[4].first()
    gk[2].second()
    gk[5].first()
    gk[6].first()
    gv[1].second()
    gv[3].first()
    gv[2].second()
    gv[4].first()
    gk[7].first()
    gk[0].relay()
    gv[5].first()
    gv[6].first()
    gv[0].relay()
    gk[1].relay()
    gv[7].first()
    gk[3].second()
    gk[4].second()
    gk[2].relay()
    gk[6].second()
    gv[1].relay()
    gk[5].second()
    gv[3].second()
    gv[2].relay()
    gv[4].second()
    gk[0].across()
    gk[1].across()
    gk[7].second()
    gv[6].second()
    gv[0].across()
    gv[5].second()
    gk[3].relay()
    gk[0].done()
    gk[1].done()
    work.fwd(0)
    gv[1].across()
    gv[7].second()
    gk[2].across()
    gk[4].across()
    gk[5].across()
    gv[3].relay()
    gv[2].across()
    gk[6].across()
    gk[4].done()
    gk[5].done()
    work.fwd(2)
    gk[7].across()
    gv[4].across()
    gk[3].across()
    gk[6].done()
    gk[7].done()
    work.fwd(3)
    gv[5].across()
    gv[6].across()
    gk[2].done()
    gk[3].done()
    work.fwd(1)
    gv[3].across()
    work.middle()
    gv[7].across()
    work.gradv(3)
    sv[3].start()
    work.gradv(2)
    sv[2].start()
    gv[4].done()
    gv[5].done()
    work.out(2)
    gv[6].done()
    gv[7].done()
    work.out(3)
    work.gradv(1)
    sv[1].start()
    sv[3].own()
    gv[2].done()
    gv[3].done()
    work.out(1)
    sv[2].own()
    work.gradv(0)
    sv[0].start()
    sv[1].own()
    gv[0].done()
    gv[1].done()
    work.out(0)
    work.deltas()
    work.bwd(3)
    sk[3].start()
    sv[0].own()
    work.bwd(2)
    sk[2].start()
    sk[3].own()
    work.bwd(1)
    sk[1].start()
    sk[2].own()
    work.bwd(0)
    sk[0].start()
    sk[1].own()
    sv[3].turn()
    sv[2].turn()
    sv[1].turn()
    sk[0].own()
    sk[3].turn()
    sv[0].turn()
    work.write_attended()
    moves["attended"].start()
    work.self_bwd()
    sk[2].turn()
    work.write_resp_grad()
    moves["rgrad"].start()
    work.gradq()
    work.write_query_grad()
    moves["qgrad"].start()
    sk[1].turn()
    sv[3].up()
    sv[2].up()
    sv[1].up()
    sk[0].turn()
    sk[3].up()
    sk[2].up()
    sv[0].up()
    sv[0].sum()
    sk[1].up()
    sv[1].sum()
    sv[2].sum()
    sv[3].sum()
    sk[0].up()
    sk[0].sum()
    sk[1].sum()
    sk[2].sum()
    sk[3].sum()
    for head in range(8):
        inner["pgrad"][:, head, :] = heads[head]
    moves["pgrad"].start()
    net.finish()
    for name in OUTPUTS:
        moves[name].wait()


def hand_on(*refs):
    sems, held, refs = refs[-1], refs[-5:-1], refs[:-5]
    inward = [pltpu.make_async_copy(refs[i], held[i], sems.at[i]) for i in range(4)]
    outward = [pltpu.make_async_copy(held[i], refs[4 + i], sems.at[4 + i]) for i in range(4)]
    for copy in inward:
        copy.start()
    for before, after in zip(inward, outward):
        before.wait()
        after.start()
    for copy in outward:
        copy.wait()


def local(queries, resp_kv, prompt_kv, resp_prompt, row_segment, cotangent):
    anywhere = pl.BlockSpec(memory_space=pl.ANY)
    shapes = (
        jax.ShapeDtypeStruct((ROWS, NH * HD), BF),
        jax.ShapeDtypeStruct((ROWS, NH * HD), BF),
        jax.ShapeDtypeStruct((ROWS, 2 * HD), BF),
        jax.ShapeDtypeStruct((SLAB, 8, 2 * HD), F32),
    )
    results = pl.pallas_call(
        kernel,
        out_shape=shapes,
        in_specs=[anywhere] * 5 + [pl.BlockSpec(memory_space=pltpu.SMEM)],
        out_specs=[anywhere] * 4,
        scratch_shapes=[shape for _, shape in SCRATCH],
        compiler_params=pltpu.CompilerParams(
            collective_id=0, has_side_effects=True, vmem_limit_bytes=56 << 20
        ),
    )(queries, cotangent, resp_kv[:, 0], prompt_kv, row_segment, resp_prompt)
    attended, query_grad, resp_grad, prompt_grad = pl.pallas_call(
        hand_on,
        out_shape=shapes,
        in_specs=[anywhere] * 4,
        out_specs=[anywhere] * 4,
        scratch_shapes=[pltpu.VMEM(shape.shape, shape.dtype) for shape in shapes] + [pltpu.SemaphoreType.DMA((8,))],
    )(*results)
    return attended, query_grad, resp_grad[:, None], prompt_grad


def solution(mesh):
    return jax.shard_map(
        local,
        mesh=mesh,
        in_specs=(
            P("dp", "tensor"),
            P("dp", "tensor", None),
            P(("dp", "tensor"), None, None),
            P("dp", None),
            P("dp", None),
            P("dp", "tensor"),
        ),
        out_specs=(
            P("dp", "tensor"),
            P("dp", "tensor"),
            P("dp", "tensor", None),
            P(("dp", "tensor"), None, None),
        ),
        check_vma=False,
    )
```

```python
import math

import jax
import jax.numpy as jnp
from jax import lax
from jax.experimental import pallas as pl
from jax.experimental.pallas import tpu as pltpu
from jax.sharding import PartitionSpec as P

MESH = pl.DeviceIdType.MESH
HD = 128
NH = 8
ROWS = 128
WIN = 64
RESP = 4
WL = NH * WIN
NCH = 4
CK = 256
BLK = 64
SLAB = 32
OFFS = (0, 1, 7, 2, 6, 3, 5, 4)
GATHER_MERGED = (1, 2)
GATHER_RELAYED = (0, 1, 2, 3)
SCATTER_MERGED = (1,)
SCALE = 1.0 / math.sqrt(HD)
ALPHA = SCALE * math.log2(math.e)
BF = jnp.bfloat16
F32 = jnp.float32


def dot(a, b):
    return jnp.dot(a, b, preferred_element_type=F32)


def dot_t(a, b):
    return lax.dot_general(a, b, (((1,), (1,)), ((), ())), preferred_element_type=F32)


class Work:
    def __init__(self, **refs):
        self.__dict__.update(refs)

    def prep(self):
        seg = self.seg[...].astype(F32)
        pos = lax.broadcasted_iota(jnp.int32, (1, ROWS), 1).astype(F32)
        for i in range(1, RESP):
            start = jnp.sum(jnp.where(seg < i, 1.0, 0.0), axis=1, keepdims=True)
            before = jnp.sum(jnp.where(seg < i - 1, 1.0, 0.0), axis=1, keepdims=True)
            pos = pos - jnp.where(seg >= i, start - before, 0.0)
        slot = seg * WIN + pos
        col = seg * (2 * WIN) + pos
        place = lax.broadcasted_iota(jnp.int32, (RESP * WIN, ROWS), 0).astype(F32)
        gather = jnp.where(place == slot, 1.0, 0.0).astype(BF)
        self.kvself[...] = dot(gather, self.rkv[...]).astype(BF)
        slot_t = jnp.broadcast_to(slot, (ROWS, ROWS)).T
        col_t = jnp.broadcast_to(col, (ROWS, ROWS)).T
        lane = lax.broadcasted_iota(jnp.int32, (ROWS, ROWS), 1).astype(F32)
        for i in range(RESP):
            here = lane + 128.0 * i
            self.spread[0:ROWS, i * 128 : (i + 1) * 128] = jnp.where(here == col_t, 1.0, 0.0).astype(BF)
            self.spread[ROWS : 2 * ROWS, i * 128 : (i + 1) * 128] = jnp.where(
                here == col_t + WIN, 1.0, 0.0
            ).astype(BF)
        for i in range(2):
            self.back[:, i * 128 : (i + 1) * 128] = jnp.where(lane + 128.0 * i == slot_t, 1.0, 0.0).astype(BF)
        spread = self.spread[...]
        for source, target in ((self.q, self.qt), (self.g, self.gt)):
            for pair in range(NH // 2):
                two = source[:, pair * 256 : (pair + 1) * 256]
                turned = jnp.concatenate([two[:, :HD].T, two[:, HD:].T], axis=1)
                placed = dot(turned, spread).astype(BF)
                for i in range(RESP):
                    target[i, :, pair * 128 : (pair + 1) * 128] = placed[:, i * 128 : (i + 1) * 128]

    def self_fwd(self):
        key = lax.broadcasted_iota(jnp.int32, (WIN, WL), 0)
        row = lax.broadcasted_iota(jnp.int32, (WIN, WL), 1) & (WIN - 1)
        seen = key <= row

        def body(i, carry):
            k = self.kvself[pl.ds(pl.multiple_of(i * WIN, WIN), WIN), 0:HD]
            s = jnp.where(seen, dot(k, self.qt[i]), -1e30)
            m = jnp.max(s, axis=0, keepdims=True)
            e = jnp.exp2((s - m) * ALPHA)
            self.wself[i] = e.astype(BF)
            self.mself[i] = m
            self.accm[i] = m
            self.accl[i] = jnp.sum(e, axis=0, keepdims=True)
            return carry

        lax.fori_loop(0, RESP, body, 0, unroll=True)

    def piece(self, bufs, j, i):
        p = self.rp[0, i]
        return bufs[j][lax.shift_right_logical(p, 1), pl.ds((p & 1) * 2, 2)].reshape(CK, HD)

    def fwd(self, j):
        def body(i, carry):
            s = dot(self.piece(self.kb, j, i), self.qt[i])
            m = jnp.max(s, axis=0, keepdims=True)
            e = jnp.exp2((s - m) * ALPHA)
            self.weight[j, i] = e.astype(BF)
            self.mbuf[j, i] = m
            old = self.accm[i]
            new = jnp.maximum(old, m)
            self.accl[i] = self.accl[i] * jnp.exp2((old - new) * ALPHA) + jnp.sum(
                e, axis=0, keepdims=True
            ) * jnp.exp2((m - new) * ALPHA)
            self.accm[i] = new
            return carry

        lax.fori_loop(0, RESP, body, 0, unroll=True)

    def middle(self):
        def body(i, carry):
            lse = self.accm[i] * ALPHA + jnp.log2(self.accl[i])
            self.lse[i] = lse
            weight = (self.wself[i].astype(F32) * jnp.exp2(self.mself[i] * ALPHA - lse)).astype(BF)
            self.wself[i] = weight
            v = self.kvself[pl.ds(pl.multiple_of(i * WIN, WIN), WIN), HD : 2 * HD]
            self.acco[i] = dot(v.T, weight)
            return carry

        lax.fori_loop(0, RESP, body, 0, unroll=True)

    def gradv(self, j):
        def body(i, carry):
            weight = self.weight[j, i].astype(F32) * jnp.exp2(self.mbuf[j, i] * ALPHA - self.lse[i])
            weight = weight.astype(BF)
            self.weight[j, i] = weight
            self.grads["v"][j][i] = dot_t(weight, self.gt[i]).astype(BF).reshape(4, BLK, HD)
            return carry

        lax.fori_loop(0, RESP, body, 0, unroll=True)

    def out(self, j):
        def body(i, carry):
            self.acco[i] = self.acco[i] + dot(self.piece(self.vb, j, i).T, self.weight[j, i])
            return carry

        lax.fori_loop(0, RESP, body, 0, unroll=True)

    def deltas(self):
        def body(i, carry):
            out = self.acco[i]
            self.delta[i] = jnp.sum(self.gt[i].astype(F32) * out, axis=0, keepdims=True)
            self.outt[i] = out.astype(BF)
            return carry

        lax.fori_loop(0, RESP, body, 0, unroll=True)

    def dscore(self, i, v, weight):
        return (weight.astype(F32) * (dot(v, self.gt[i]) - self.delta[i])).astype(BF)

    def self_bwd(self):
        def body(i, carry):
            at = pl.ds(pl.multiple_of(i * WIN, WIN), WIN)
            kv = self.kvself[at, :]
            ds = self.dscore(i, kv[:, HD:], self.wself[i])
            dk = dot_t(ds, self.qt[i]) * SCALE
            dv = dot_t(self.wself[i], self.gt[i])
            self.dself[at, :] = jnp.concatenate([dk, dv], axis=1).astype(BF)
            self.dqt[i] = dot(kv[:, :HD].T, ds)
            return carry

        lax.fori_loop(0, RESP, body, 0, unroll=True)

    def bwd(self, j):
        def body(i, carry):
            ds = self.dscore(i, self.piece(self.vb, j, i), self.weight[j, i])
            self.grads["k"][j][i] = (dot_t(ds, self.qt[i]) * SCALE).astype(BF).reshape(4, BLK, HD)
            self.weight[j, i] = ds
            return carry

        lax.fori_loop(0, RESP, body, 0, unroll=True)

    def gradq(self):
        def body(i, carry):
            total = self.dqt[i]
            for j in range(NCH):
                total = total + dot(self.piece(self.kb, j, i).T, self.weight[j, i])
            self.dqt[i] = total
            return carry

        lax.fori_loop(0, RESP, body, 0, unroll=True)

    def place_rows(self, source, scale, target):
        for head in range(NH):
            at = pl.ds((head // 2) * 128, 128)
            parts = [source[i, :, at] for i in range(RESP)]
            if scale is not None:
                parts = [part * scale for part in parts]
            whole = jnp.concatenate([part.astype(BF) for part in parts], axis=1)
            rows = self.spread[(head % 2) * ROWS : (head % 2 + 1) * ROWS, :]
            target[:, head * HD : (head + 1) * HD] = dot_t(rows, whole).astype(BF)

    def write_attended(self):
        self.place_rows(self.outt, None, self.attended)

    def write_query_grad(self):
        self.place_rows(self.dqt, SCALE, self.qgrad)

    def write_resp_grad(self):
        self.rgrad[...] = dot(self.back[...], self.dself[...]).astype(BF)

    def selected(self, kind, j, p, part):
        total = None
        for i in range(RESP):
            mine = jnp.where(self.rp[0, i] == p, 1.0, 0.0).astype(BF)
            term = self.grads[kind][j][i, part] * mine
            total = term if total is None else total + term
        return total


WORK_SCRATCH = dict(
    kvself=pltpu.VMEM((RESP * WIN, 2 * HD), BF),
    spread=pltpu.VMEM((2 * ROWS, RESP * 128), BF),
    back=pltpu.VMEM((ROWS, RESP * WIN), BF),
    qt=pltpu.VMEM((RESP, HD, WL), BF),
    gt=pltpu.VMEM((RESP, HD, WL), BF),
    wself=pltpu.VMEM((RESP, WIN, WL), BF),
    weight=pltpu.VMEM((NCH, RESP, CK, WL), BF),
    mself=pltpu.VMEM((RESP, 1, WL), F32),
    mbuf=pltpu.VMEM((NCH, RESP, 1, WL), F32),
    accm=pltpu.VMEM((RESP, 1, WL), F32),
    accl=pltpu.VMEM((RESP, 1, WL), F32),
    lse=pltpu.VMEM((RESP, 1, WL), F32),
    delta=pltpu.VMEM((RESP, 1, WL), F32),
    acco=pltpu.VMEM((RESP, HD, WL), F32),
    outt=pltpu.VMEM((RESP, HD, WL), BF),
    dqt=pltpu.VMEM((RESP, HD, WL), F32),
    dself=pltpu.VMEM((RESP * WIN, 2 * HD), BF),
)


class Batch:
    def __init__(self, whole, sem):
        self.whole = pltpu.make_async_copy(whole, whole, sem)

    def wait_recv(self):
        self.whole.wait()


class Net:
    def __init__(self, send_sem, recv_sem):
        self.dp, self.t = lax.axis_index("dp"), lax.axis_index("tensor")
        self.x, self.y, self.c = self.dp // 8, (self.dp // 2) % 4, self.dp % 2
        self.send_sem, self.recv_sem = send_sem, recv_sem
        self.count = self.taken = 0
        self.sent = []

    def at(self, axis):
        return self.x if axis == "x" else self.y

    def device(self, axis=None, step=0, up=0, other=False):
        x = (self.x + step) % 4 if axis == "x" else self.x
        y = (self.y + step) % 4 if axis == "y" else self.y
        c = 1 - self.c if other else self.c
        return (x * 8 + y * 2 + c, (self.t + up) % 8)

    def batch(self, whole, copies):
        shared = self.taken
        self.taken += 1
        for src, dst, device in copies:
            self.copy(src, dst, device, shared)
        return Batch(whole, self.recv_sem.at[shared])

    def copy(self, src, dst, device, shared=None):
        index = self.count
        self.count += 1
        if shared is None:
            shared = self.taken
            self.taken += 1
        if index >= SENDS:
            self.sent[index - SENDS].wait_send()
        made = pltpu.make_async_remote_copy(
            src_ref=src,
            dst_ref=dst,
            send_sem=self.send_sem.at[index % SENDS],
            recv_sem=self.recv_sem.at[shared],
            device_id=device,
            device_id_type=MESH,
        )
        made.start()
        self.sent.append(made)
        return made

    def greet(self, targets):
        barrier = pltpu.get_barrier_semaphore()
        for axis, step, up, other in targets:
            pl.semaphore_signal(
                barrier, inc=1, device_id=self.device(axis, 4 - step, 8 - up, other), device_id_type=MESH
            )

    def greeted(self, targets):
        pl.semaphore_wait(pltpu.get_barrier_semaphore(), len(targets))

    def finish(self):
        for made in self.sent[-SENDS:]:
            made.wait_send()


def first_axis(place):
    return "xy"[place % 2]


def second_axis(place):
    return "yx"[place % 2]


def targets():
    found = {(None, 0, 0, True)}
    for axis in "xy":
        found.update((axis, step, 0, False) for step in (1, 2, 3))
    for place in range(1, 8):
        for merged, up in ((GATHER_MERGED, -OFFS[place] % 8), (SCATTER_MERGED, OFFS[place])):
            found.add((None, 0, up, False))
            if place in merged:
                found.update((first_axis(place), step, up, False) for step in (1, 2, 3))
    return sorted(found, key=str)


class Gather:
    def __init__(self, net, place, buf):
        self.net, self.place, self.buf = net, place, buf
        self.low = (place % 2) * SLAB

    def line(self, axis, at, low=0, size=SLAB):
        rows = pl.ds(self.low + low, size)
        if axis == "x":
            return self.buf.at[at, :, self.net.c, rows]
        return self.buf.at[:, at, self.net.c, rows]

    def mine(self):
        net = self.net
        return self.buf.at[net.x, net.y, net.c, pl.ds(self.low, SLAB)]

    def row(self, src, count, devices):
        whole = self.buf.at[0, 0:count, self.net.c, pl.ds(self.low, SLAB)]
        return self.net.batch(whole, [(src, self.mine(), device) for device in devices])

    def up(self, slabs):
        net, place, axis = self.net, self.place, first_axis(self.place)
        away = -OFFS[place] % 8
        slab = slabs.at[(net.t + away) % 8]
        self.arrived = None
        if place == 0:
            self.buf[net.x, net.y, net.c, 0:SLAB] = slab[...]
            self.lined = self.row(slab, 3, [net.device(axis, step) for step in (1, 2, 3)])
        elif place in GATHER_MERGED:
            self.lined = self.row(slab, 4, [net.device(axis, step, away) for step in (1, 2, 3, 0)])
        else:
            self.arrived = net.copy(slab, self.mine(), net.device(None, 0, away))

    def first(self):
        if self.arrived is not None:
            net, axis = self.net, first_axis(self.place)
            self.arrived.wait_recv()
            self.lined = self.row(self.mine(), 3, [net.device(axis, step) for step in (1, 2, 3)])

    def second(self):
        net, axis = self.net, second_axis(self.place)
        self.lined.wait_recv()
        line = self.line(axis, net.at(axis))
        if self.place in GATHER_RELAYED:
            self.lines = [net.copy(line, line, net.device(axis, step)) for step in (1, 3)]
        else:
            whole = self.buf.at[0:3, :, net.c, pl.ds(self.low, SLAB)]
            self.lines = [net.batch(whole, [(line, line, net.device(axis, step)) for step in (1, 2, 3)])]

    def relay(self):
        if self.place in GATHER_RELAYED:
            net, axis = self.net, second_axis(self.place)
            handed = []
            for way, step in enumerate((1, 3)):
                self.lines[way].wait_recv()
                part = self.line(axis, (net.at(axis) + 4 - step) % 4, way * (SLAB // 2), SLAB // 2)
                handed.append(net.copy(part, part, net.device(axis, step)))
            self.lines = handed

    def across(self):
        net = self.net
        for made in self.lines:
            made.wait_recv()
        held = self.buf.at[:, :, net.c, pl.ds(self.low, SLAB)]
        self.sibling = net.copy(held, held, net.device(other=True))

    def done(self):
        self.sibling.wait_recv()


class Scatter:
    def __init__(self, net, work, kind, j, refs, final, heads):
        self.net, self.work, self.kind, self.j, self.final, self.heads = net, work, kind, j, final, heads
        self.__dict__.update(refs)

    def start(self):
        net = self.net

        def body(p, carry):
            for half in (0, 1):
                value = self.work.selected(self.kind, self.j, p, 2 * half + (1 - net.c))
                self.give[p // 2, (p % 2) * 2 + half] = value
            return carry

        lax.fori_loop(0, 8, body, 0, unroll=4)
        self.sibling = net.copy(self.give, self.take, net.device(other=True))

    def line(self, half, axis, at):
        rows = pl.ds(half * SLAB, SLAB)
        return self.held.at[at, :, rows] if axis == "x" else self.held.at[:, at, rows]

    def own(self):
        net = self.net
        self.sibling.wait_recv()

        def body(p, carry):
            for half in (0, 1):
                x, y = p // 2, (p % 2) * 2 + half
                value = self.work.selected(self.kind, self.j, p, 2 * half + net.c)
                self.held[x, y] = (value.astype(F32) + self.take[x, y].astype(F32)).astype(BF)
            return carry

        lax.fori_loop(0, 8, body, 0, unroll=4)
        self.lined = []
        for half in (0, 1):
            axis = second_axis(half)
            copies = [
                (
                    self.line(half, axis, (net.at(axis) + step) % 4),
                    self.came.at[half, step - 1],
                    net.device(axis, step),
                )
                for step in (1, 2, 3)
            ]
            self.lined.append(net.batch(self.came.at[half], copies))

    def turn(self):
        net = self.net
        self.homeward = []
        for half in (0, 1):
            axis = second_axis(half)
            total = self.line(half, axis, net.at(axis))[...].astype(F32)
            self.lined[half].wait_recv()
            for index in range(3):
                total = total + self.came[half, index].astype(F32)
            self.rest[half] = total.astype(BF)
            place, axis = 2 * self.j + half, first_axis(half)
            away = OFFS[place] if place in SCATTER_MERGED else 0
            copies = []
            for step in (1, 2, 3, 0):
                src, dst = self.rest.at[half, (net.at(axis) + step) % 4], self.final.at[place, step]
                if away == 0 and step == 0:
                    self.final[place, 0] = src[...]
                else:
                    copies.append((src, dst, net.device(axis, step, away)))
            whole = self.final.at[place, 4 - len(copies) : 4]
            self.homeward.append(net.batch(whole, copies))

    def summed(self, place, half):
        self.homeward[half].wait_recv()
        total = self.final[place, 0].astype(F32)
        for step in (1, 2, 3):
            total = total + self.final[place, step].astype(F32)
        return total

    def up(self):
        net = self.net
        self.last = [None, None]
        for half in (0, 1):
            place = 2 * self.j + half
            if OFFS[place] != 0 and place not in SCATTER_MERGED:
                self.ready[half] = self.summed(place, half).astype(BF)
                self.last[half] = net.copy(
                    self.ready.at[half], self.came_up.at[half], net.device(None, 0, OFFS[place])
                )

    def sum(self):
        net = self.net
        for half in (0, 1):
            place = 2 * self.j + half
            head = (net.t + 8 - OFFS[place]) % 8
            lanes = slice(0, HD) if self.kind == "k" else slice(HD, 2 * HD)
            if self.last[half] is None:
                self.heads[head, :, lanes] = self.summed(place, half)
            else:
                self.last[half].wait_recv()
                self.heads[head, :, lanes] = self.came_up[half].astype(F32)


SCATTER_SCRATCH = dict(
    give=pltpu.VMEM((4, 4, BLK, HD), BF),
    take=pltpu.VMEM((4, 4, BLK, HD), BF),
    held=pltpu.VMEM((4, 4, BLK, HD), BF),
    came=pltpu.VMEM((2, 3, 4, SLAB, HD), BF),
    rest=pltpu.VMEM((2, 4, SLAB, HD), BF),
    ready=pltpu.VMEM((2, SLAB, HD), BF),
    came_up=pltpu.VMEM((2, SLAB, HD), BF),
)
RECEIVES = 134
SENDS = 64
SCRATCH = (
    [("send_sem", pltpu.SemaphoreType.DMA((SENDS,))), ("recv_sem", pltpu.SemaphoreType.DMA((RECEIVES,)))]
    + [("kb", pltpu.VMEM((4, 4, 2, BLK, HD), BF)), ("vb", pltpu.VMEM((4, 4, 2, BLK, HD), BF))] * NCH
    + [("dk", pltpu.VMEM((RESP, 4, BLK, HD), BF)), ("dv", pltpu.VMEM((RESP, 4, BLK, HD), BF))] * NCH
    + [
        ("kslabs", pltpu.VMEM((8, SLAB, HD), BF)),
        ("vslabs", pltpu.VMEM((8, SLAB, HD), BF)),
        ("wide", pltpu.VMEM((2, SLAB * 8, HD), F32)),
        ("final", pltpu.VMEM((8, 4, SLAB, HD), BF)),
        ("final", pltpu.VMEM((8, 4, SLAB, HD), BF)),
        ("near_sem", pltpu.SemaphoreType.DMA((9,))),
        ("q", pltpu.VMEM((ROWS, NH * HD), BF)),
        ("g", pltpu.VMEM((ROWS, NH * HD), BF)),
        ("rkv", pltpu.VMEM((ROWS, 2 * HD), BF)),
        ("pkv", pltpu.VMEM((SLAB, 8, 2 * HD), BF)),
        ("seg", pltpu.VMEM((1, ROWS), jnp.int32)),
        ("attended", pltpu.VMEM((ROWS, NH * HD), BF)),
        ("qgrad", pltpu.VMEM((ROWS, NH * HD), BF)),
        ("rgrad", pltpu.VMEM((ROWS, 2 * HD), BF)),
        ("heads", pltpu.VMEM((8, SLAB, 2 * HD), F32)),
        ("pgrad", pltpu.VMEM((SLAB, 8, 2 * HD), F32)),
    ]
    + list(WORK_SCRATCH.items())
    + list(SCATTER_SCRATCH.items()) * (2 * NCH)
)


INPUTS = ("pkv", "q", "g", "rkv", "seg")
OUTPUTS = ("attended", "qgrad", "rgrad", "pgrad")


def kernel(q, g, rkv, pkv, seg, rp, attended, qgrad, rgrad, pgrad, *scratch):
    outer = dict(q=q, g=g, rkv=rkv, pkv=pkv, seg=seg, attended=attended, qgrad=qgrad, rgrad=rgrad, pgrad=pgrad)
    named = {}
    for (name, _), ref in zip(SCRATCH, scratch):
        named.setdefault(name, []).append(ref)
    inner = {name: named[name][0] for name in outer}
    refs = {name: named[name][0] for name in WORK_SCRATCH}
    work = Work(rp=rp, kb=named["kb"], vb=named["vb"], grads=dict(k=named["dk"], v=named["dv"]), **inner, **refs)
    near_sem = named["near_sem"][0]
    moves = {}
    for index, name in enumerate(INPUTS):
        moves[name] = pltpu.make_async_copy(outer[name], inner[name], near_sem.at[index])
    for index, name in enumerate(OUTPUTS):
        moves[name] = pltpu.make_async_copy(inner[name], outer[name], near_sem.at[len(INPUTS) + index])
    moves["pkv"].start()
    net = Net(named["send_sem"][0], named["recv_sem"][0])
    slabs = dict(k=named["kslabs"][0], v=named["vslabs"][0])
    wide, heads = named["wide"][0], named["heads"][0]
    gk = [Gather(net, place, named["kb"][place // 2]) for place in range(8)]
    gv = [Gather(net, place, named["vb"][place // 2]) for place in range(8)]
    scatters = []
    for index in range(2 * NCH):
        scratch_of = {name: named[name][index] for name in SCATTER_SCRATCH}
        kind, j = "kv"[index // NCH], index % NCH
        scatters.append(Scatter(net, work, kind, j, scratch_of, named["final"][index // NCH], heads))
    sk, sv = scatters[:NCH], scatters[NCH:]
    net.greet(targets())
    for name in INPUTS[1:]:
        moves[name].start()
    moves["pkv"].wait()
    pkv = inner["pkv"]
    for part in (0, 1):
        wide[part] = pkv[:, :, part * HD : (part + 1) * HD].astype(F32).reshape(SLAB * 8, HD)
    for head in range(8):
        for part in (0, 1):
            slabs["kv"[part]][head] = wide[part, pl.ds(head, SLAB, stride=8), :].astype(BF)
    net.greeted(targets())
    for gather in gk:
        gather.up(slabs["k"])
    for gather in gv:
        gather.up(slabs["v"])
    for name in INPUTS[1:]:
        moves[name].wait()
    work.prep()
    work.self_fwd()
    gk[0].second()
    gv[0].second()
    gk[1].second()
    gk[3].first()
    gk[4].first()
    gk[2].second()
    gk[5].first()
    gk[6].first()
    gv[1].second()
    gv[3].first()
    gv[2].second()
    gv[4].first()
    gk[7].first()
    gk[0].relay()
    gv[5].first()
    gv[6].first()
    gv[0].relay()
    gk[1].relay()
    gv[7].first()
    gk[3].second()
    gk[4].second()
    gk[2].relay()
    gk[6].second()
    gv[1].relay()
    gk[5].second()
    gv[3].second()
    gv[2].relay()
    gv[4].second()
    gk[0].across()
    gk[1].across()
    gk[7].second()
    gv[6].second()
    gv[0].across()
    gv[5].second()
    gk[3].relay()
    gk[0].done()
    gk[1].done()
    work.fwd(0)
    gv[1].across()
    gv[7].second()
    gk[2].across()
    gk[4].across()
    gk[5].across()
    gv[3].relay()
    gv[2].across()
    gk[6].across()
    gk[4].done()
    gk[5].done()
    work.fwd(2)
    gk[7].across()
    gv[4].across()
    gk[3].across()
    gk[6].done()
    gk[7].done()
    work.fwd(3)
    gv[5].across()
    gv[6].across()
    gk[2].done()
    gk[3].done()
    work.fwd(1)
    gv[3].across()
    work.middle()
    gv[7].across()
    work.gradv(3)
    sv[3].start()
    work.gradv(2)
    sv[2].start()
    gv[4].done()
    gv[5].done()
    work.out(2)
    gv[6].done()
    gv[7].done()
    work.out(3)
    work.gradv(1)
    sv[1].start()
    sv[3].own()
    gv[2].done()
    gv[3].done()
    work.out(1)
    sv[2].own()
    work.gradv(0)
    sv[0].start()
    sv[1].own()
    gv[0].done()
    gv[1].done()
    work.out(0)
    work.deltas()
    work.bwd(3)
    sk[3].start()
    sv[0].own()
    work.bwd(2)
    sk[2].start()
    sk[3].own()
    work.bwd(1)
    sk[1].start()
    sk[2].own()
    work.bwd(0)
    sk[0].start()
    sk[1].own()
    sv[3].turn()
    sv[2].turn()
    sv[1].turn()
    sk[0].own()
    sk[3].turn()
    sv[0].turn()
    work.write_attended()
    moves["attended"].start()
    work.self_bwd()
    sk[2].turn()
    work.write_resp_grad()
    moves["rgrad"].start()
    work.gradq()
    work.write_query_grad()
    moves["qgrad"].start()
    sk[1].turn()
    sv[3].up()
    sv[2].up()
    sv[1].up()
    sk[0].turn()
    sk[3].up()
    sk[2].up()
    sv[0].up()
    sv[0].sum()
    sk[1].up()
    sv[1].sum()
    sv[2].sum()
    sv[3].sum()
    sk[0].up()
    sk[0].sum()
    sk[1].sum()
    sk[2].sum()
    sk[3].sum()
    for head in range(8):
        inner["pgrad"][:, head, :] = heads[head]
    moves["pgrad"].start()
    net.finish()
    for name in OUTPUTS:
        moves[name].wait()


def hand_on(*refs):
    sems, held, refs = refs[-1], refs[-5:-1], refs[:-5]
    inward = [pltpu.make_async_copy(refs[i], held[i], sems.at[i]) for i in range(4)]
    outward = [pltpu.make_async_copy(held[i], refs[4 + i], sems.at[4 + i]) for i in range(4)]
    for copy in inward:
        copy.start()
    for before, after in zip(inward, outward):
        before.wait()
        after.start()
    for copy in outward:
        copy.wait()


def local(queries, resp_kv, prompt_kv, resp_prompt, row_segment, cotangent):
    anywhere = pl.BlockSpec(memory_space=pl.ANY)
    shapes = (
        jax.ShapeDtypeStruct((ROWS, NH * HD), BF),
        jax.ShapeDtypeStruct((ROWS, NH * HD), BF),
        jax.ShapeDtypeStruct((ROWS, 2 * HD), BF),
        jax.ShapeDtypeStruct((SLAB, 8, 2 * HD), F32),
    )
    results = pl.pallas_call(
        kernel,
        out_shape=shapes,
        in_specs=[anywhere] * 5 + [pl.BlockSpec(memory_space=pltpu.SMEM)],
        out_specs=[anywhere] * 4,
        scratch_shapes=[shape for _, shape in SCRATCH],
        compiler_params=pltpu.CompilerParams(
            collective_id=0, has_side_effects=True, vmem_limit_bytes=56 << 20
        ),
    )(queries, cotangent, resp_kv[:, 0], prompt_kv, row_segment, resp_prompt)
    attended, query_grad, resp_grad, prompt_grad = pl.pallas_call(
        hand_on,
        out_shape=shapes,
        in_specs=[anywhere] * 4,
        out_specs=[anywhere] * 4,
        scratch_shapes=[pltpu.VMEM(shape.shape, shape.dtype) for shape in shapes] + [pltpu.SemaphoreType.DMA((8,))],
    )(*results)
    return attended, query_grad, resp_grad[:, None], prompt_grad


def solution(mesh):
    return jax.shard_map(
        local,
        mesh=mesh,
        in_specs=(
            P("dp", "tensor"),
            P("dp", "tensor", None),
            P(("dp", "tensor"), None, None),
            P("dp", None),
            P("dp", None),
            P("dp", "tensor"),
        ),
        out_specs=(
            P("dp", "tensor"),
            P("dp", "tensor"),
            P("dp", "tensor", None),
            P(("dp", "tensor"), None, None),
        ),
        check_vma=False,
    )
```

```python
import math

import jax
import jax.numpy as jnp
from jax import lax
from jax.experimental import pallas as pl
from jax.experimental.pallas import tpu as pltpu
from jax.sharding import PartitionSpec as P

MESH = pl.DeviceIdType.MESH
HD = 128
NH = 8
ROWS = 128
WIN = 64
RESP = 4
WL = NH * WIN
NCH = 4
CK = 256
BLK = 64
SLAB = 32
OFFS = (0, 1, 7, 2, 6, 3, 5, 4)
GATHER_MERGED = (1, 2)
GATHER_RELAYED = (0, 1, 2, 3)
SCATTER_MERGED = (1,)
SCALE = 1.0 / math.sqrt(HD)
ALPHA = SCALE * math.log2(math.e)
BF = jnp.bfloat16
F32 = jnp.float32


def dot(a, b):
    return jnp.dot(a, b, preferred_element_type=F32)


def dot_t(a, b):
    return lax.dot_general(a, b, (((1,), (1,)), ((), ())), preferred_element_type=F32)


class Work:
    def __init__(self, **refs):
        self.__dict__.update(refs)

    def prep(self):
        seg = self.seg[...].astype(F32)
        pos = lax.broadcasted_iota(jnp.int32, (1, ROWS), 1).astype(F32)
        for i in range(1, RESP):
            start = jnp.sum(jnp.where(seg < i, 1.0, 0.0), axis=1, keepdims=True)
            before = jnp.sum(jnp.where(seg < i - 1, 1.0, 0.0), axis=1, keepdims=True)
            pos = pos - jnp.where(seg >= i, start - before, 0.0)
        slot = seg * WIN + pos
        col = seg * (2 * WIN) + pos
        place = lax.broadcasted_iota(jnp.int32, (RESP * WIN, ROWS), 0).astype(F32)
        gather = jnp.where(place == slot, 1.0, 0.0).astype(BF)
        self.kvself[...] = dot(gather, self.rkv[...]).astype(BF)
        slot_t = jnp.broadcast_to(slot, (ROWS, ROWS)).T
        col_t = jnp.broadcast_to(col, (ROWS, ROWS)).T
        lane = lax.broadcasted_iota(jnp.int32, (ROWS, ROWS), 1).astype(F32)
        for i in range(RESP):
            here = lane + 128.0 * i
            self.spread[0:ROWS, i * 128 : (i + 1) * 128] = jnp.where(here == col_t, 1.0, 0.0).astype(BF)
            self.spread[ROWS : 2 * ROWS, i * 128 : (i + 1) * 128] = jnp.where(
                here == col_t + WIN, 1.0, 0.0
            ).astype(BF)
        for i in range(2):
            self.back[:, i * 128 : (i + 1) * 128] = jnp.where(lane + 128.0 * i == slot_t, 1.0, 0.0).astype(BF)
        spread = self.spread[...]
        for source, target in ((self.q, self.qt), (self.g, self.gt)):
            for pair in range(NH // 2):
                two = source[:, pair * 256 : (pair + 1) * 256]
                turned = jnp.concatenate([two[:, :HD].T, two[:, HD:].T], axis=1)
                placed = dot(turned, spread).astype(BF)
                for i in range(RESP):
                    target[i, :, pair * 128 : (pair + 1) * 128] = placed[:, i * 128 : (i + 1) * 128]

    def self_fwd(self):
        key = lax.broadcasted_iota(jnp.int32, (WIN, WL), 0)
        row = lax.broadcasted_iota(jnp.int32, (WIN, WL), 1) & (WIN - 1)
        seen = key <= row

        def body(i, carry):
            k = self.kvself[pl.ds(pl.multiple_of(i * WIN, WIN), WIN), 0:HD]
            s = jnp.where(seen, dot(k, self.qt[i]), -1e30)
            m = jnp.max(s, axis=0, keepdims=True)
            e = jnp.exp2((s - m) * ALPHA)
            self.wself[i] = e.astype(BF)
            self.mself[i] = m
            self.accm[i] = m
            self.accl[i] = jnp.sum(e, axis=0, keepdims=True)
            return carry

        lax.fori_loop(0, RESP, body, 0, unroll=True)

    def piece(self, bufs, j, i):
        p = self.rp[0, i]
        return bufs[j][lax.shift_right_logical(p, 1), pl.ds((p & 1) * 2, 2)].reshape(CK, HD)

    def fwd(self, j):
        def body(i, carry):
            s = dot(self.piece(self.kb, j, i), self.qt[i])
            m = jnp.max(s, axis=0, keepdims=True)
            e = jnp.exp2((s - m) * ALPHA)
            self.weight[j, i] = e.astype(BF)
            self.mbuf[j, i] = m
            old = self.accm[i]
            new = jnp.maximum(old, m)
            self.accl[i] = self.accl[i] * jnp.exp2((old - new) * ALPHA) + jnp.sum(
                e, axis=0, keepdims=True
            ) * jnp.exp2((m - new) * ALPHA)
            self.accm[i] = new
            return carry

        lax.fori_loop(0, RESP, body, 0, unroll=True)

    def middle(self):
        def body(i, carry):
            lse = self.accm[i] * ALPHA + jnp.log2(self.accl[i])
            self.lse[i] = lse
            weight = (self.wself[i].astype(F32) * jnp.exp2(self.mself[i] * ALPHA - lse)).astype(BF)
            self.wself[i] = weight
            v = self.kvself[pl.ds(pl.multiple_of(i * WIN, WIN), WIN), HD : 2 * HD]
            self.acco[i] = dot(v.T, weight)
            return carry

        lax.fori_loop(0, RESP, body, 0, unroll=True)

    def gradv(self, j):
        def body(i, carry):
            weight = self.weight[j, i].astype(F32) * jnp.exp2(self.mbuf[j, i] * ALPHA - self.lse[i])
            weight = weight.astype(BF)
            self.weight[j, i] = weight
            self.grads["v"][j][i] = dot_t(weight, self.gt[i]).astype(BF).reshape(4, BLK, HD)
            return carry

        lax.fori_loop(0, RESP, body, 0, unroll=True)

    def out(self, j):
        def body(i, carry):
            self.acco[i] = self.acco[i] + dot(self.piece(self.vb, j, i).T, self.weight[j, i])
            return carry

        lax.fori_loop(0, RESP, body, 0, unroll=True)

    def deltas(self):
        def body(i, carry):
            out = self.acco[i]
            self.delta[i] = jnp.sum(self.gt[i].astype(F32) * out, axis=0, keepdims=True)
            self.outt[i] = out.astype(BF)
            return carry

        lax.fori_loop(0, RESP, body, 0, unroll=True)

    def dscore(self, i, v, weight):
        return (weight.astype(F32) * (dot(v, self.gt[i]) - self.delta[i])).astype(BF)

    def self_bwd(self):
        def body(i, carry):
            at = pl.ds(pl.multiple_of(i * WIN, WIN), WIN)
            kv = self.kvself[at, :]
            ds = self.dscore(i, kv[:, HD:], self.wself[i])
            dk = dot_t(ds, self.qt[i]) * SCALE
            dv = dot_t(self.wself[i], self.gt[i])
            self.dself[at, :] = jnp.concatenate([dk, dv], axis=1).astype(BF)
            self.dqt[i] = dot(kv[:, :HD].T, ds)
            return carry

        lax.fori_loop(0, RESP, body, 0, unroll=True)

    def bwd(self, j):
        def body(i, carry):
            ds = self.dscore(i, self.piece(self.vb, j, i), self.weight[j, i])
            self.grads["k"][j][i] = (dot_t(ds, self.qt[i]) * SCALE).astype(BF).reshape(4, BLK, HD)
            self.weight[j, i] = ds
            return carry

        lax.fori_loop(0, RESP, body, 0, unroll=True)

    def gradq(self):
        def body(i, carry):
            total = self.dqt[i]
            for j in range(NCH):
                total = total + dot(self.piece(self.kb, j, i).T, self.weight[j, i])
            self.dqt[i] = total
            return carry

        lax.fori_loop(0, RESP, body, 0, unroll=True)

    def place_rows(self, source, scale, target):
        for head in range(NH):
            at = pl.ds((head // 2) * 128, 128)
            parts = [source[i, :, at] for i in range(RESP)]
            if scale is not None:
                parts = [part * scale for part in parts]
            whole = jnp.concatenate([part.astype(BF) for part in parts], axis=1)
            rows = self.spread[(head % 2) * ROWS : (head % 2 + 1) * ROWS, :]
            target[:, head * HD : (head + 1) * HD] = dot_t(rows, whole).astype(BF)

    def write_attended(self):
        self.place_rows(self.outt, None, self.attended)

    def write_query_grad(self):
        self.place_rows(self.dqt, SCALE, self.qgrad)

    def write_resp_grad(self):
        self.rgrad[...] = dot(self.back[...], self.dself[...]).astype(BF)

    def selected(self, kind, j, p, part):
        total = None
        for i in range(RESP):
            mine = jnp.where(self.rp[0, i] == p, 1.0, 0.0).astype(BF)
            term = self.grads[kind][j][i, part] * mine
            total = term if total is None else total + term
        return total


WORK_SCRATCH = dict(
    kvself=pltpu.VMEM((RESP * WIN, 2 * HD), BF),
    spread=pltpu.VMEM((2 * ROWS, RESP * 128), BF),
    back=pltpu.VMEM((ROWS, RESP * WIN), BF),
    qt=pltpu.VMEM((RESP, HD, WL), BF),
    gt=pltpu.VMEM((RESP, HD, WL), BF),
    wself=pltpu.VMEM((RESP, WIN, WL), BF),
    weight=pltpu.VMEM((NCH, RESP, CK, WL), BF),
    mself=pltpu.VMEM((RESP, 1, WL), F32),
    mbuf=pltpu.VMEM((NCH, RESP, 1, WL), F32),
    accm=pltpu.VMEM((RESP, 1, WL), F32),
    accl=pltpu.VMEM((RESP, 1, WL), F32),
    lse=pltpu.VMEM((RESP, 1, WL), F32),
    delta=pltpu.VMEM((RESP, 1, WL), F32),
    acco=pltpu.VMEM((RESP, HD, WL), F32),
    outt=pltpu.VMEM((RESP, HD, WL), BF),
    dqt=pltpu.VMEM((RESP, HD, WL), F32),
    dself=pltpu.VMEM((RESP * WIN, 2 * HD), BF),
)


class Batch:
    def __init__(self, whole, sem):
        self.whole = pltpu.make_async_copy(whole, whole, sem)

    def wait_recv(self):
        self.whole.wait()


class Net:
    def __init__(self, send_sem, recv_sem):
        self.dp, self.t = lax.axis_index("dp"), lax.axis_index("tensor")
        self.x, self.y, self.c = self.dp // 8, (self.dp // 2) % 4, self.dp % 2
        self.send_sem, self.recv_sem = send_sem, recv_sem
        self.count = self.taken = 0
        self.sent = []

    def at(self, axis):
        return self.x if axis == "x" else self.y

    def device(self, axis=None, step=0, up=0, other=False):
        x = (self.x + step) % 4 if axis == "x" else self.x
        y = (self.y + step) % 4 if axis == "y" else self.y
        c = 1 - self.c if other else self.c
        return (x * 8 + y * 2 + c, (self.t + up) % 8)

    def batch(self, whole, copies):
        shared = self.taken
        self.taken += 1
        for src, dst, device in copies:
            self.copy(src, dst, device, shared)
        return Batch(whole, self.recv_sem.at[shared])

    def copy(self, src, dst, device, shared=None):
        index = self.count
        self.count += 1
        if shared is None:
            shared = self.taken
            self.taken += 1
        if index >= SENDS:
            self.sent[index - SENDS].wait_send()
        made = pltpu.make_async_remote_copy(
            src_ref=src,
            dst_ref=dst,
            send_sem=self.send_sem.at[index % SENDS],
            recv_sem=self.recv_sem.at[shared],
            device_id=device,
            device_id_type=MESH,
        )
        made.start()
        self.sent.append(made)
        return made

    def greet(self, targets):
        barrier = pltpu.get_barrier_semaphore()
        for axis, step, up, other in targets:
            pl.semaphore_signal(
                barrier, inc=1, device_id=self.device(axis, 4 - step, 8 - up, other), device_id_type=MESH
            )

    def greeted(self, targets):
        pl.semaphore_wait(pltpu.get_barrier_semaphore(), len(targets))

    def finish(self):
        for made in self.sent[-SENDS:]:
            made.wait_send()


def first_axis(place):
    return "xy"[place % 2]


def second_axis(place):
    return "yx"[place % 2]


def targets():
    found = {(None, 0, 0, True)}
    for axis in "xy":
        found.update((axis, step, 0, False) for step in (1, 2, 3))
    for place in range(1, 8):
        for merged, up in ((GATHER_MERGED, -OFFS[place] % 8), (SCATTER_MERGED, OFFS[place])):
            found.add((None, 0, up, False))
            if place in merged:
                found.update((first_axis(place), step, up, False) for step in (1, 2, 3))
    return sorted(found, key=str)


class Gather:
    def __init__(self, net, place, buf):
        self.net, self.place, self.buf = net, place, buf
        self.low = (place % 2) * SLAB

    def line(self, axis, at, low=0, size=SLAB):
        rows = pl.ds(self.low + low, size)
        if axis == "x":
            return self.buf.at[at, :, self.net.c, rows]
        return self.buf.at[:, at, self.net.c, rows]

    def mine(self):
        net = self.net
        return self.buf.at[net.x, net.y, net.c, pl.ds(self.low, SLAB)]

    def row(self, src, count, devices):
        whole = self.buf.at[0, 0:count, self.net.c, pl.ds(self.low, SLAB)]
        return self.net.batch(whole, [(src, self.mine(), device) for device in devices])

    def up(self, slabs):
        net, place, axis = self.net, self.place, first_axis(self.place)
        away = -OFFS[place] % 8
        slab = slabs.at[(net.t + away) % 8]
        self.arrived = None
        if place == 0:
            self.buf[net.x, net.y, net.c, 0:SLAB] = slab[...]
            self.lined = self.row(slab, 3, [net.device(axis, step) for step in (1, 2, 3)])
        elif place in GATHER_MERGED:
            self.lined = self.row(slab, 4, [net.device(axis, step, away) for step in (1, 2, 3, 0)])
        else:
            self.arrived = net.copy(slab, self.mine(), net.device(None, 0, away))

    def first(self):
        if self.arrived is not None:
            net, axis = self.net, first_axis(self.place)
            self.arrived.wait_recv()
            self.lined = self.row(self.mine(), 3, [net.device(axis, step) for step in (1, 2, 3)])

    def second(self):
        net, axis = self.net, second_axis(self.place)
        self.lined.wait_recv()
        line = self.line(axis, net.at(axis))
        if self.place in GATHER_RELAYED:
            self.lines = [net.copy(line, line, net.device(axis, step)) for step in (1, 3)]
        else:
            whole = self.buf.at[0:3, :, net.c, pl.ds(self.low, SLAB)]
            self.lines = [net.batch(whole, [(line, line, net.device(axis, step)) for step in (1, 2, 3)])]

    def relay(self):
        if self.place in GATHER_RELAYED:
            net, axis = self.net, second_axis(self.place)
            handed = []
            for way, step in enumerate((1, 3)):
                self.lines[way].wait_recv()
                part = self.line(axis, (net.at(axis) + 4 - step) % 4, way * (SLAB // 2), SLAB // 2)
                handed.append(net.copy(part, part, net.device(axis, step)))
            self.lines = handed

    def across(self):
        net = self.net
        for made in self.lines:
            made.wait_recv()
        held = self.buf.at[:, :, net.c, pl.ds(self.low, SLAB)]
        self.sibling = net.copy(held, held, net.device(other=True))

    def done(self):
        self.sibling.wait_recv()


class Scatter:
    def __init__(self, net, work, kind, j, refs, final, heads):
        self.net, self.work, self.kind, self.j, self.final, self.heads = net, work, kind, j, final, heads
        self.__dict__.update(refs)

    def start(self):
        net = self.net

        def body(p, carry):
            for half in (0, 1):
                value = self.work.selected(self.kind, self.j, p, 2 * half + (1 - net.c))
                self.give[p // 2, (p % 2) * 2 + half] = value
            return carry

        lax.fori_loop(0, 8, body, 0, unroll=4)
        self.sibling = net.copy(self.give, self.take, net.device(other=True))

    def line(self, half, axis, at):
        rows = pl.ds(half * SLAB, SLAB)
        return self.held.at[at, :, rows] if axis == "x" else self.held.at[:, at, rows]

    def own(self):
        net = self.net
        self.sibling.wait_recv()

        def body(p, carry):
            for half in (0, 1):
                x, y = p // 2, (p % 2) * 2 + half
                value = self.work.selected(self.kind, self.j, p, 2 * half + net.c)
                self.held[x, y] = (value.astype(F32) + self.take[x, y].astype(F32)).astype(BF)
            return carry

        lax.fori_loop(0, 8, body, 0, unroll=4)
        self.lined = []
        for half in (0, 1):
            axis = second_axis(half)
            copies = [
                (
                    self.line(half, axis, (net.at(axis) + step) % 4),
                    self.came.at[half, step - 1],
                    net.device(axis, step),
                )
                for step in (1, 2, 3)
            ]
            self.lined.append(net.batch(self.came.at[half], copies))

    def turn(self):
        net = self.net
        self.homeward = []
        for half in (0, 1):
            axis = second_axis(half)
            total = self.line(half, axis, net.at(axis))[...].astype(F32)
            self.lined[half].wait_recv()
            for index in range(3):
                total = total + self.came[half, index].astype(F32)
            self.rest[half] = total.astype(BF)
            place, axis = 2 * self.j + half, first_axis(half)
            away = OFFS[place] if place in SCATTER_MERGED else 0
            copies = []
            for step in (1, 2, 3, 0):
                src, dst = self.rest.at[half, (net.at(axis) + step) % 4], self.final.at[place, step]
                if away == 0 and step == 0:
                    self.final[place, 0] = src[...]
                else:
                    copies.append((src, dst, net.device(axis, step, away)))
            whole = self.final.at[place, 4 - len(copies) : 4]
            self.homeward.append(net.batch(whole, copies))

    def summed(self, place, half):
        self.homeward[half].wait_recv()
        total = self.final[place, 0].astype(F32)
        for step in (1, 2, 3):
            total = total + self.final[place, step].astype(F32)
        return total

    def up(self):
        net = self.net
        self.last = [None, None]
        for half in (0, 1):
            place = 2 * self.j + half
            if OFFS[place] != 0 and place not in SCATTER_MERGED:
                self.ready[half] = self.summed(place, half).astype(BF)
                self.last[half] = net.copy(
                    self.ready.at[half], self.came_up.at[half], net.device(None, 0, OFFS[place])
                )

    def sum(self):
        net = self.net
        for half in (0, 1):
            place = 2 * self.j + half
            head = (net.t + 8 - OFFS[place]) % 8
            lanes = slice(0, HD) if self.kind == "k" else slice(HD, 2 * HD)
            if self.last[half] is None:
                self.heads[head, :, lanes] = self.summed(place, half)
            else:
                self.last[half].wait_recv()
                self.heads[head, :, lanes] = self.came_up[half].astype(F32)


SCATTER_SCRATCH = dict(
    give=pltpu.VMEM((4, 4, BLK, HD), BF),
    take=pltpu.VMEM((4, 4, BLK, HD), BF),
    held=pltpu.VMEM((4, 4, BLK, HD), BF),
    came=pltpu.VMEM((2, 3, 4, SLAB, HD), BF),
    rest=pltpu.VMEM((2, 4, SLAB, HD), BF),
    ready=pltpu.VMEM((2, SLAB, HD), BF),
    came_up=pltpu.VMEM((2, SLAB, HD), BF),
)
RECEIVES = 134
SENDS = 32
SCRATCH = (
    [("send_sem", pltpu.SemaphoreType.DMA((SENDS,))), ("recv_sem", pltpu.SemaphoreType.DMA((RECEIVES,)))]
    + [("kb", pltpu.VMEM((4, 4, 2, BLK, HD), BF)), ("vb", pltpu.VMEM((4, 4, 2, BLK, HD), BF))] * NCH
    + [("dk", pltpu.VMEM((RESP, 4, BLK, HD), BF)), ("dv", pltpu.VMEM((RESP, 4, BLK, HD), BF))] * NCH
    + [
        ("kslabs", pltpu.VMEM((8, SLAB, HD), BF)),
        ("vslabs", pltpu.VMEM((8, SLAB, HD), BF)),
        ("wide", pltpu.VMEM((2, SLAB * 8, HD), F32)),
        ("final", pltpu.VMEM((8, 4, SLAB, HD), BF)),
        ("final", pltpu.VMEM((8, 4, SLAB, HD), BF)),
        ("near_sem", pltpu.SemaphoreType.DMA((9,))),
        ("q", pltpu.VMEM((ROWS, NH * HD), BF)),
        ("g", pltpu.VMEM((ROWS, NH * HD), BF)),
        ("rkv", pltpu.VMEM((ROWS, 2 * HD), BF)),
        ("pkv", pltpu.VMEM((SLAB, 8, 2 * HD), BF)),
        ("seg", pltpu.VMEM((1, ROWS), jnp.int32)),
        ("attended", pltpu.VMEM((ROWS, NH * HD), BF)),
        ("qgrad", pltpu.VMEM((ROWS, NH * HD), BF)),
        ("rgrad", pltpu.VMEM((ROWS, 2 * HD), BF)),
        ("heads", pltpu.VMEM((8, SLAB, 2 * HD), F32)),
        ("pgrad", pltpu.VMEM((SLAB, 8, 2 * HD), F32)),
    ]
    + list(WORK_SCRATCH.items())
    + list(SCATTER_SCRATCH.items()) * (2 * NCH)
)


INPUTS = ("pkv", "q", "g", "rkv", "seg")
OUTPUTS = ("attended", "qgrad", "rgrad", "pgrad")


def kernel(q, g, rkv, pkv, seg, rp, attended, qgrad, rgrad, pgrad, *scratch):
    outer = dict(q=q, g=g, rkv=rkv, pkv=pkv, seg=seg, attended=attended, qgrad=qgrad, rgrad=rgrad, pgrad=pgrad)
    named = {}
    for (name, _), ref in zip(SCRATCH, scratch):
        named.setdefault(name, []).append(ref)
    inner = {name: named[name][0] for name in outer}
    refs = {name: named[name][0] for name in WORK_SCRATCH}
    work = Work(rp=rp, kb=named["kb"], vb=named["vb"], grads=dict(k=named["dk"], v=named["dv"]), **inner, **refs)
    near_sem = named["near_sem"][0]
    moves = {}
    for index, name in enumerate(INPUTS):
        moves[name] = pltpu.make_async_copy(outer[name], inner[name], near_sem.at[index])
    for index, name in enumerate(OUTPUTS):
        moves[name] = pltpu.make_async_copy(inner[name], outer[name], near_sem.at[len(INPUTS) + index])
    moves["pkv"].start()
    net = Net(named["send_sem"][0], named["recv_sem"][0])
    slabs = dict(k=named["kslabs"][0], v=named["vslabs"][0])
    wide, heads = named["wide"][0], named["heads"][0]
    gk = [Gather(net, place, named["kb"][place // 2]) for place in range(8)]
    gv = [Gather(net, place, named["vb"][place // 2]) for place in range(8)]
    scatters = []
    for index in range(2 * NCH):
        scratch_of = {name: named[name][index] for name in SCATTER_SCRATCH}
        kind, j = "kv"[index // NCH], index % NCH
        scatters.append(Scatter(net, work, kind, j, scratch_of, named["final"][index // NCH], heads))
    sk, sv = scatters[:NCH], scatters[NCH:]
    net.greet(targets())
    for name in INPUTS[1:]:
        moves[name].start()
    moves["pkv"].wait()
    pkv = inner["pkv"]
    for part in (0, 1):
        wide[part] = pkv[:, :, part * HD : (part + 1) * HD].astype(F32).reshape(SLAB * 8, HD)
    for head in range(8):
        for part in (0, 1):
            slabs["kv"[part]][head] = wide[part, pl.ds(head, SLAB, stride=8), :].astype(BF)
    net.greeted(targets())
    for gather in gk:
        gather.up(slabs["k"])
    for gather in gv:
        gather.up(slabs["v"])
    for name in INPUTS[1:]:
        moves[name].wait()
    work.prep()
    work.self_fwd()
    gk[0].second()
    gv[0].second()
    gk[1].second()
    gk[3].first()
    gk[4].first()
    gk[2].second()
    gk[5].first()
    gk[6].first()
    gv[1].second()
    gv[3].first()
    gv[2].second()
    gv[4].first()
    gk[7].first()
    gk[0].relay()
    gv[5].first()
    gv[6].first()
    gv[0].relay()
    gk[1].relay()
    gv[7].first()
    gk[3].second()
    gk[4].second()
    gk[2].relay()
    gk[6].second()
    gv[1].relay()
    gk[5].second()
    gv[3].second()
    gv[2].relay()
    gv[4].second()
    gk[0].across()
    gk[1].across()
    gk[7].second()
    gv[6].second()
    gv[0].across()
    gv[5].second()
    gk[3].relay()
    gk[0].done()
    gk[1].done()
    work.fwd(0)
    gv[1].across()
    gv[7].second()
    gk[2].across()
    gk[4].across()
    gk[5].across()
    gv[3].relay()
    gv[2].across()
    gk[6].across()
    gk[4].done()
    gk[5].done()
    work.fwd(2)
    gk[7].across()
    gv[4].across()
    gk[3].across()
    gk[6].done()
    gk[7].done()
    work.fwd(3)
    gv[5].across()
    gv[6].across()
    gk[2].done()
    gk[3].done()
    work.fwd(1)
    gv[3].across()
    work.middle()
    gv[7].across()
    work.gradv(3)
    sv[3].start()
    work.gradv(2)
    sv[2].start()
    gv[4].done()
    gv[5].done()
    work.out(2)
    gv[6].done()
    gv[7].done()
    work.out(3)
    work.gradv(1)
    sv[1].start()
    sv[3].own()
    gv[2].done()
    gv[3].done()
    work.out(1)
    sv[2].own()
    work.gradv(0)
    sv[0].start()
    sv[1].own()
    gv[0].done()
    gv[1].done()
    work.out(0)
    work.deltas()
    work.bwd(3)
    sk[3].start()
    sv[0].own()
    work.bwd(2)
    sk[2].start()
    sk[3].own()
    work.bwd(1)
    sk[1].start()
    sk[2].own()
    work.bwd(0)
    sk[0].start()
    sk[1].own()
    sv[3].turn()
    sv[2].turn()
    sv[1].turn()
    sk[0].own()
    sk[3].turn()
    sv[0].turn()
    work.write_attended()
    moves["attended"].start()
    work.self_bwd()
    sk[2].turn()
    work.write_resp_grad()
    moves["rgrad"].start()
    work.gradq()
    work.write_query_grad()
    moves["qgrad"].start()
    sk[1].turn()
    sv[3].up()
    sv[2].up()
    sv[1].up()
    sk[0].turn()
    sk[3].up()
    sk[2].up()
    sv[0].up()
    sv[0].sum()
    sk[1].up()
    sv[1].sum()
    sv[2].sum()
    sv[3].sum()
    sk[0].up()
    sk[0].sum()
    sk[1].sum()
    sk[2].sum()
    sk[3].sum()
    for head in range(8):
        inner["pgrad"][:, head, :] = heads[head]
    moves["pgrad"].start()
    net.finish()
    for name in OUTPUTS:
        moves[name].wait()


def hand_on(*refs):
    sems, held, refs = refs[-1], refs[-5:-1], refs[:-5]
    inward = [pltpu.make_async_copy(refs[i], held[i], sems.at[i]) for i in range(4)]
    outward = [pltpu.make_async_copy(held[i], refs[4 + i], sems.at[4 + i]) for i in range(4)]
    for copy in inward:
        copy.start()
    for before, after in zip(inward, outward):
        before.wait()
        after.start()
    for copy in outward:
        copy.wait()


def local(queries, resp_kv, prompt_kv, resp_prompt, row_segment, cotangent):
    anywhere = pl.BlockSpec(memory_space=pl.ANY)
    shapes = (
        jax.ShapeDtypeStruct((ROWS, NH * HD), BF),
        jax.ShapeDtypeStruct((ROWS, NH * HD), BF),
        jax.ShapeDtypeStruct((ROWS, 2 * HD), BF),
        jax.ShapeDtypeStruct((SLAB, 8, 2 * HD), F32),
    )
    results = pl.pallas_call(
        kernel,
        out_shape=shapes,
        in_specs=[anywhere] * 5 + [pl.BlockSpec(memory_space=pltpu.SMEM)],
        out_specs=[anywhere] * 4,
        scratch_shapes=[shape for _, shape in SCRATCH],
        compiler_params=pltpu.CompilerParams(
            collective_id=0, has_side_effects=True, vmem_limit_bytes=56 << 20
        ),
    )(queries, cotangent, resp_kv[:, 0], prompt_kv, row_segment, resp_prompt)
    attended, query_grad, resp_grad, prompt_grad = pl.pallas_call(
        hand_on,
        out_shape=shapes,
        in_specs=[anywhere] * 4,
        out_specs=[anywhere] * 4,
        scratch_shapes=[pltpu.VMEM(shape.shape, shape.dtype) for shape in shapes] + [pltpu.SemaphoreType.DMA((8,))],
    )(*results)
    return attended, query_grad, resp_grad[:, None], prompt_grad


def solution(mesh):
    return jax.shard_map(
        local,
        mesh=mesh,
        in_specs=(
            P("dp", "tensor"),
            P("dp", "tensor", None),
            P(("dp", "tensor"), None, None),
            P("dp", None),
            P("dp", None),
            P("dp", "tensor"),
        ),
        out_specs=(
            P("dp", "tensor"),
            P("dp", "tensor"),
            P("dp", "tensor", None),
            P(("dp", "tensor"), None, None),
        ),
        check_vma=False,
    )
```
